32 devices in a mesh: dp: 8 (over z, core), ctx: 4 (over y, x).
Axes of the slice: x: 2, y: 2, z: 4, core: 2. Of those that a mesh axis runs over, the one named last changes fastest.
Arguments:
- inputs: bfloat16 [4096, 8192], P(('dp', 'ctx')), may hold values from -6 to 6
- out_grad: bfloat16 [4096, 8192], P(('dp', 'ctx')), may hold values from -6 to 6
- queries: bfloat16 [4096, 1024], P(('dp', 'ctx')), may hold values from -9 to 9
- keys: bfloat16 [4096, 128], P(('dp', 'ctx')), may hold values from -9 to 9
- values: bfloat16 [4096, 128], P(('dp', 'ctx')), may hold values from -6 to 6
- attn_grad: bfloat16 [4096, 1024], P(('dp', 'ctx')), may hold values from -6 to 6
- doc_lengths: int32 [8, 12], P('dp'), may hold values from 1 to 256, 512 in all within a row
- block_owner: int32 [8, 16], P('dp'), may hold values from 0 to 3, as said below
- basis_qkv: bfloat16 [8192, 512], P('ctx'), may hold values from -0.0625 to 0.0625
- basis_out: bfloat16 [8192, 512], P('ctx'), may hold values from -0.0625 to 0.0625
Outputs:
- grad_queries: bfloat16 [4096, 1024], P(('dp', 'ctx'))
- grad_keys: bfloat16 [4096, 128], P(('dp', 'ctx'))
- grad_values: bfloat16 [4096, 128], P(('dp', 'ctx'))
- galore_qkv: float32 [512, 1280], P(('dp', 'ctx'))
- galore_out: float32 [512, 1024], P(('dp', 'ctx'))
The draws below stay inside these ranges and needn't reach their ends.
Inputs may be any that keep to these rules, and one draw needn't show every extreme that they name: `block_owner`: in each window every ctx device is named by exactly 4 blocks, and by at most one of the 4 consecutive blocks of any one device.
All inputs are finite; a program needn't handle non-finite values.
Results may differ from the reference program's by a relative error of at most 0.018.
Values may be sent and summed in bfloat16 or wider, within the bound.
A program may use at most 128 MiB of HBM per device.

```python
import math
import jax
import jax.numpy as jnp
import numpy as np
from jax import lax

D = 8192
HD = 128
HQ = 8
GROUPS = 1
RANK = 512
BPD = 4
NDOC = 12
BLK = 32
WINDOW = 512
WINDOWS = 8
TOKENS = 4096
NBLK = 16
MOST = 256


def draw_queries(key, part):
    key = jax.random.fold_in(key, 17)
    drawn = jnp.clip(jax.random.normal(key, (TOKENS, GROUPS * HQ, HD), jnp.float32), -6.0, 6.0)
    return drawn.reshape(TOKENS, GROUPS * HQ * HD).astype(jnp.bfloat16)


def draw_keys(key, part):
    key = jax.random.fold_in(key, 29)
    drawn = jnp.clip(jax.random.normal(key, (TOKENS, GROUPS, HD), jnp.float32), -6.0, 6.0)
    return drawn.reshape(TOKENS, GROUPS * HD).astype(jnp.bfloat16)


def draw_block_owner(key, part):
    key = jax.random.fold_in(key, 41)
    peer_count = NBLK // BPD
    window_keys = jax.random.split(key, WINDOWS)

    def one_window(window_key):
        offset_key, order_key = jax.random.split(window_key)
        offsets = jax.random.permutation(offset_key, peer_count)[:BPD]
        source_keys = jax.random.split(order_key, peer_count)
        orders = jax.vmap(lambda source_key: jax.random.permutation(source_key, BPD))(source_keys)
        chosen = jnp.take(offsets, orders)
        sources = jnp.arange(peer_count, dtype=jnp.int32)[:, None]
        return ((sources + chosen) % peer_count).reshape(NBLK).astype(jnp.int32)
    return jax.vmap(one_window)(window_keys)


def block_scale(own_key, shape, cuts, smallest, top_value):
    factor_of = 1.0
    for position, blocks in cuts:
        draws = jax.random.uniform(jax.random.fold_in(jax.random.fold_in(own_key, 6), position), (blocks,), jnp.float32, smallest / len(cuts), top_value / len(cuts))
        factor_of = factor_of * jnp.repeat(jnp.exp(draws), shape[position] // blocks).reshape((-1,) + (1,) * (len(shape) - 1 - position))
    return factor_of


def profile(number_of, total, bound, lean):
    portions = [(1 << 20) // math.isqrt(standing ** lean) + 1 for standing in range(2, number_of + 1)]
    rest, counts = total - bound - (number_of - 1), [1] * (number_of - 1)
    while rest > 0:
        candidates = [i for i in range(number_of - 1) if counts[i] < bound]
        whole, budget = sum([portions[i] for i in candidates]), rest
        for i in candidates:
            extra = min(bound - counts[i], max(1, budget * portions[i] // whole), rest)
            counts[i] = counts[i] + extra
            rest = rest - extra
    return np.array([bound] + counts)


def uneven(key, amount, total, reach, slope):
    if amount == 2:
        one = jax.random.randint(key, (), max(1, total - reach), min(reach, total - 1) + 1)
        return jnp.stack([one, total - one])
    tallies = jnp.asarray(profile(amount, total, reach, slope), jnp.int32)
    couples = (amount - 1) // 2
    giver, sink = tallies[1:1 + 2 * couples:2], tallies[2:2 + 2 * couples:2]
    room = jnp.minimum(giver - 1, reach - sink)
    moved = jax.random.randint(jax.random.fold_in(key, 1), (couples,), 0, 1 << 20) % (room + 1)
    tallies = tallies.at[1:1 + 2 * couples:2].set(giver - moved).at[2:2 + 2 * couples:2].set(sink + moved)
    return tallies[jax.random.permutation(jax.random.fold_in(key, 2), amount)]


def scatter_about(rng, extent, deviation, most, cuts=(), kind=jnp.bfloat16):
    level = block_scale(rng, extent, cuts, -0.22, 0.18) if cuts else 1.0
    values = jax.random.normal(rng, extent, jnp.float32) * deviation * level
    return jnp.minimum(jnp.maximum(values, -most), most).astype(kind)


def setup_inputs(seed: int = 0) -> dict:
    streams_of = jax.random.split(jax.random.key(seed), 11)
    inputs = scatter_about(streams_of[0], (TOKENS, D), 1.0, 6.0, ((0, 32),))
    out_grad = scatter_about(streams_of[1], (TOKENS, D), 1.0, 6.0, ((0, 32),))
    queries = draw_queries(jax.random.fold_in(streams_of[10], 71), 0)
    keys = draw_keys(jax.random.fold_in(streams_of[10], 71), 0)
    values = scatter_about(streams_of[4], (TOKENS, GROUPS * HD), 1.0, 6.0, ((0, 32),))
    attn_grad = scatter_about(streams_of[5], (TOKENS, GROUPS * HQ * HD), 1.0, 6.0, ((0, 32),))
    doc_lengths = jax.vmap(lambda own: uneven(own, NDOC, WINDOW, MOST, 2))(jax.random.split(streams_of[6], WINDOWS)).reshape((WINDOWS, NDOC)).astype(jnp.int32)
    block_owner = draw_block_owner(jax.random.fold_in(streams_of[10], 71), 0)
    basis_qkv = scatter_about(streams_of[8], (D, RANK), D ** -0.5, 0.0625, ((0, 4),))
    basis_out = scatter_about(streams_of[9], (D, RANK), D ** -0.5, 0.0625, ((0, 4),))
    return dict(inputs=inputs, out_grad=out_grad, queries=queries, keys=keys, values=values, attn_grad=attn_grad, doc_lengths=doc_lengths, block_owner=block_owner, basis_qkv=basis_qkv, basis_out=basis_out)


def document_index(lengths_row, positions):
    doc_ends = jnp.cumsum(lengths_row).astype(jnp.int32)
    return jnp.sum((positions[:, None] >= doc_ends[None, :]).astype(jnp.int32), axis=1)


def window_attention(query_win, key_win, value_win, dout_win, lengths_row):
    scale_factor = HD ** -0.5
    positions = jnp.arange(WINDOW, dtype=jnp.int32)
    key_docs = document_index(lengths_row, positions)
    key_wide = key_win.astype(jnp.float32)
    value_wide = value_win.astype(jnp.float32)

    def one_block(running, block_id):
        grad_key, grad_value = running
        first_pos = (block_id * BLK).astype(jnp.int32)
        query_blk = lax.dynamic_slice_in_dim(query_win, first_pos, BLK, 0).astype(jnp.float32)
        dout_blk = lax.dynamic_slice_in_dim(dout_win, first_pos, BLK, 0).astype(jnp.float32)
        query_pos = first_pos + jnp.arange(BLK, dtype=jnp.int32)
        query_docs = lax.dynamic_slice_in_dim(key_docs, first_pos, BLK, 0)
        allowed = (query_docs[:, None] == key_docs[None, :]) & (positions[None, :] <= query_pos[:, None])
        allowed = allowed[:, None, :]
        scores = jnp.einsum("thd,kd->thk", query_blk, key_wide) * scale_factor
        peak_score = jnp.max(jnp.where(allowed, scores, -jnp.inf), axis=-1, keepdims=True)
        denom_total = jnp.sum(jnp.where(allowed, jnp.exp(scores - peak_score), 0.0), axis=-1, keepdims=True)
        log_total = peak_score + jnp.log(denom_total)
        probability = jnp.where(allowed, jnp.exp(scores - log_total), 0.0)
        weights_wide = lax.optimization_barrier(probability.astype(jnp.bfloat16)).astype(jnp.float32)
        attn_block = jnp.einsum("thk,kd->thd", weights_wide, value_wide).astype(jnp.bfloat16)
        out_wide = lax.optimization_barrier(attn_block).astype(jnp.float32)
        row_delta = jnp.sum(dout_blk * out_wide, axis=-1, keepdims=True)
        grad_prob = jnp.einsum("thd,kd->thk", dout_blk, value_wide)
        grad_scores = probability * (grad_prob - row_delta) * scale_factor
        grad_wide = lax.optimization_barrier(grad_scores.astype(jnp.bfloat16)).astype(jnp.float32)
        grad_query = jnp.einsum("thk,kd->thd", grad_wide, key_wide).astype(jnp.bfloat16)
        grad_key = grad_key + jnp.einsum("thk,thd->kd", grad_wide, query_blk)
        grad_value = grad_value + jnp.einsum("thk,thd->kd", weights_wide, dout_blk)
        return (grad_key, grad_value), (grad_query, attn_block)

    start_state = (jnp.zeros((WINDOW, HD), jnp.float32), jnp.zeros((WINDOW, HD), jnp.float32))
    block_ids = jnp.arange(WINDOW // BLK, dtype=jnp.int32)
    (grad_key, grad_value), (grad_query, attn_out) = lax.scan(one_block, start_state, block_ids)
    return (grad_query.reshape(WINDOW, HQ * HD), attn_out.reshape(WINDOW, HQ * HD),
            grad_key.astype(jnp.bfloat16), grad_value.astype(jnp.bfloat16))


def reference(inputs, out_grad, queries, keys, values, attn_grad, doc_lengths, block_owner, basis_qkv, basis_out):
    natural_list, regrouped_list, out_list, key_list, value_list = [], [], [], [], []
    for window_id in range(WINDOWS):
        begin_row = window_id * WINDOW
        query_win = queries[begin_row:begin_row + WINDOW].reshape(WINDOW, GROUPS, HQ, HD)
        dout_win = attn_grad[begin_row:begin_row + WINDOW].reshape(WINDOW, GROUPS, HQ, HD)
        key_win = keys[begin_row:begin_row + WINDOW].reshape(WINDOW, GROUPS, HD)
        value_win = values[begin_row:begin_row + WINDOW].reshape(WINDOW, GROUPS, HD)
        group_query, group_out, group_key, group_value = [], [], [], []
        for group_id in range(GROUPS):
            grad_q_part, out_part, grad_k_part, grad_v_part = window_attention(
                query_win[:, group_id], key_win[:, group_id], value_win[:, group_id],
                dout_win[:, group_id], doc_lengths[window_id])
            group_query.append(grad_q_part)
            group_out.append(out_part)
            group_key.append(grad_k_part)
            group_value.append(grad_v_part)
        natural_win = jnp.concatenate(group_query, axis=1)
        natural_list.append(natural_win)
        out_list.append(jnp.concatenate(group_out, axis=1))
        key_list.append(jnp.concatenate(group_key, axis=1))
        value_list.append(jnp.concatenate(group_value, axis=1))
        sort_keys = block_owner[window_id].astype(jnp.int32) * NBLK + jnp.arange(NBLK, dtype=jnp.int32)
        block_order = jnp.argsort(sort_keys).astype(jnp.int32)
        moved = natural_win.reshape(NBLK, BLK, GROUPS * HQ * HD)[block_order]
        regrouped_list.append(moved.reshape(WINDOW, GROUPS * HQ * HD))
    grad_natural = jnp.concatenate(natural_list, axis=0)
    grad_queries = jnp.concatenate(regrouped_list, axis=0)
    attn_out = jnp.concatenate(out_list, axis=0)
    grad_keys = jnp.concatenate(key_list, axis=0)
    grad_values = jnp.concatenate(value_list, axis=0)
    input_proj = jnp.dot(inputs, basis_qkv, preferred_element_type=jnp.float32).astype(jnp.bfloat16)
    grad_proj = jnp.dot(out_grad, basis_out, preferred_element_type=jnp.float32).astype(jnp.bfloat16)
    norm_factor = TOKENS ** -0.5
    galore_qkv = jnp.concatenate([
        jnp.dot(input_proj.T, grad_natural, preferred_element_type=jnp.float32),
        jnp.dot(input_proj.T, grad_keys, preferred_element_type=jnp.float32),
        jnp.dot(input_proj.T, grad_values, preferred_element_type=jnp.float32)], axis=1) * norm_factor
    galore_out = jnp.dot(grad_proj.T, attn_out, preferred_element_type=jnp.float32) * norm_factor
    return grad_queries, grad_keys, grad_values, galore_qkv, galore_out
```

```python
import functools
import math

import jax
import jax.numpy as jnp
from jax import lax
from jax.experimental import pallas as pl
from jax.experimental.pallas import tpu as pltpu
from jax.sharding import PartitionSpec as P

HD = 128
HQ = 8
GROUPS = 1
BPD = 4


NEG_LARGE = -1e30


def doc_index_of(ends_row, positions):
    return jnp.sum((positions[:, None] >= ends_row[None, :]).astype(jnp.int32), axis=1)


def doc_start_of(ends_row, position):
    return jnp.max(jnp.where(ends_row <= position, ends_row, 0))


def slot_buffer(blocks, destination, peer_count):
    chooser = (destination[None, :] == jnp.arange(peer_count, dtype=jnp.int32)[:, None]).astype(
        blocks.dtype
    )
    return jnp.einsum("dj,jbf->dbf", chooser, blocks)


def compact_slots(received, sources, peer_count):
    chooser = (sources[:, None] == jnp.arange(peer_count, dtype=jnp.int32)[None, :]).astype(
        received.dtype
    )
    return jnp.einsum("kd,dbf->kbf", chooser, received)


def attend_group(
    query_rows,
    dout_rows,
    row_pos,
    row_docs,
    low_key,
    high_key,
    key_group,
    value_group,
    key_docs,
    key_block,
    grad_key,
    grad_value,
):
    scale_factor = HD ** (-0.5)
    block_count = key_group.shape[0] // key_block
    row_count = query_rows.shape[0]
    across = (((1,), (1,)), ((), ()))
    downward = (((0,), (0,)), ((), ()))

    def block_scores(block_id):
        begin_key = block_id * key_block
        key_piece = lax.dynamic_slice_in_dim(key_group, begin_key, key_block, 0)
        value_piece = lax.dynamic_slice_in_dim(value_group, begin_key, key_block, 0)
        piece_docs = lax.dynamic_slice_in_dim(key_docs, begin_key, key_block, 0)
        key_pos = begin_key + jnp.arange(key_block, dtype=jnp.int32)
        allowed = (row_docs[:, None] == piece_docs[None, :]) & (
            key_pos[None, :] <= row_pos[:, None]
        )
        scores = (
            lax.dot_general(query_rows, key_piece, across, preferred_element_type=jnp.float32)
            * scale_factor
        )
        return (scores, allowed, key_piece, value_piece)

    def needed(block_id):
        return (block_id * key_block <= high_key) & ((block_id + 1) * key_block > low_key)

    def stats_step(block_id, running):

        def stats_compute(stats_in):
            peak_old, total_old = stats_in
            scores, allowed, key_piece, value_piece = block_scores(block_id)
            peak_new = jnp.maximum(peak_old, jnp.max(jnp.where(allowed, scores, NEG_LARGE), axis=1))
            shifted = jnp.where(allowed, jnp.exp(scores - peak_new[:, None]), 0.0)
            return (peak_new, total_old * jnp.exp(peak_old - peak_new) + jnp.sum(shifted, axis=1))

        return lax.cond(needed(block_id), stats_compute, lambda unchanged: unchanged, running)

    start_stats = (
        jnp.full((row_count,), NEG_LARGE, jnp.float32),
        jnp.zeros((row_count,), jnp.float32),
    )
    peak_score, denom_total = lax.fori_loop(0, block_count, stats_step, start_stats)
    log_total = peak_score + jnp.log(denom_total)

    def out_step(block_id, running):

        def out_compute(acc_in):
            scores, allowed, key_piece, value_piece = block_scores(block_id)
            weights = jnp.where(allowed, jnp.exp(scores - log_total[:, None]), 0.0).astype(
                jnp.bfloat16
            )
            return acc_in + jnp.dot(weights, value_piece, preferred_element_type=jnp.float32)

        return lax.cond(needed(block_id), out_compute, lambda unchanged: unchanged, running)

    out_sums = lax.fori_loop(0, block_count, out_step, jnp.zeros((row_count, HD), jnp.float32))
    out_rows = out_sums.astype(jnp.bfloat16)
    row_delta = jnp.sum(dout_rows.astype(jnp.float32) * out_rows.astype(jnp.float32), axis=1)

    def grad_step(block_id, running):

        def grad_compute(carried):
            grad_query, key_acc, value_acc = carried
            scores, allowed, key_piece, value_piece = block_scores(block_id)
            probability = jnp.where(allowed, jnp.exp(scores - log_total[:, None]), 0.0)
            weights = probability.astype(jnp.bfloat16)
            grad_prob = lax.dot_general(
                dout_rows, value_piece, across, preferred_element_type=jnp.float32
            )
            grad_scores = (probability * (grad_prob - row_delta[:, None]) * scale_factor).astype(
                jnp.bfloat16
            )
            grad_query = grad_query + jnp.dot(
                grad_scores, key_piece, preferred_element_type=jnp.float32
            )
            begin_key = block_id * key_block
            key_update = lax.dot_general(
                grad_scores, query_rows, downward, preferred_element_type=jnp.float32
            )
            value_update = lax.dot_general(
                weights, dout_rows, downward, preferred_element_type=jnp.float32
            )
            key_acc = lax.dynamic_update_slice_in_dim(
                key_acc,
                lax.dynamic_slice_in_dim(key_acc, begin_key, key_block, 0) + key_update,
                begin_key,
                0,
            )
            value_acc = lax.dynamic_update_slice_in_dim(
                value_acc,
                lax.dynamic_slice_in_dim(value_acc, begin_key, key_block, 0) + value_update,
                begin_key,
                0,
            )
            return (grad_query, key_acc, value_acc)

        return lax.cond(needed(block_id), grad_compute, lambda unchanged: unchanged, running)

    start_grads = (jnp.zeros((row_count, HD), jnp.float32), grad_key, grad_value)
    grad_query, grad_key, grad_value = lax.fori_loop(0, block_count, grad_step, start_grads)
    return (grad_query.astype(jnp.bfloat16), out_rows, grad_key, grad_value)


def attention_backward(
    query_local, dout_local, block_starts, key_all, value_all, ends_row, block_len, key_block
):
    token_count = query_local.shape[0]
    window_len = key_all.shape[0]
    key_docs = doc_index_of(ends_row, jnp.arange(window_len, dtype=jnp.int32))
    query_view = query_local.reshape(token_count, GROUPS, HQ * HD)
    dout_view = dout_local.reshape(token_count, GROUPS, HQ * HD)
    query_groups, out_groups, key_groups, value_groups = ([], [], [], [])
    grad_key = jnp.zeros((window_len, HD), jnp.float32)
    grad_value = jnp.zeros((window_len, HD), jnp.float32)
    query_blocks = []
    out_blocks = []
    for block_id in range(BPD):
        first_pos = block_starts[block_id]
        lower_row = block_id * block_len
        query_rows = query_view[lower_row : lower_row + block_len, 0].reshape(block_len * HQ, HD)
        dout_rows = dout_view[lower_row : lower_row + block_len, 0].reshape(block_len * HQ, HD)
        row_pos = jnp.repeat(first_pos + jnp.arange(block_len, dtype=jnp.int32), HQ)
        row_docs = doc_index_of(ends_row, row_pos)
        low_key = doc_start_of(ends_row, first_pos)
        high_key = first_pos + block_len - 1
        grad_rows, out_rows, grad_key, grad_value = attend_group(
            query_rows,
            dout_rows,
            row_pos,
            row_docs,
            low_key,
            high_key,
            key_all,
            value_all,
            key_docs,
            key_block,
            grad_key,
            grad_value,
        )
        query_blocks.append(grad_rows.reshape(block_len, HQ * HD))
        out_blocks.append(out_rows.reshape(block_len, HQ * HD))
    query_groups.append(jnp.concatenate(query_blocks, axis=0))
    out_groups.append(jnp.concatenate(out_blocks, axis=0))
    key_groups.append(grad_key)
    value_groups.append(grad_value)
    return (query_groups[0], out_groups[0], key_groups[0], value_groups[0])


def shards(
    inputs,
    out_grad,
    queries,
    keys,
    values,
    attn_grad,
    doc_lengths,
    block_owner,
    basis_qkv,
    basis_out,
):
    peer_count = lax.axis_size("ctx")
    self_index = lax.axis_index("ctx")
    token_count = inputs.shape[0]
    window_len = token_count * peer_count
    block_len = token_count // BPD
    key_block = min(512, window_len)
    ends_row = jnp.cumsum(doc_lengths[0])
    owners = block_owner[0]
    input_sums = jnp.dot(
        inputs,
        lax.all_gather(basis_qkv, "ctx", axis=0, tiled=True),
        preferred_element_type=jnp.float32,
    )
    grad_sums = jnp.dot(
        out_grad,
        lax.all_gather(basis_out, "ctx", axis=0, tiled=True),
        preferred_element_type=jnp.float32,
    )
    input_proj = input_sums.astype(jnp.bfloat16)
    grad_proj = grad_sums.astype(jnp.bfloat16)
    key_all, value_all = (
        lax.all_gather(keys, "ctx", axis=0, tiled=True),
        lax.all_gather(values, "ctx", axis=0, tiled=True),
    )
    owned_mask = (owners == self_index).astype(jnp.int32)
    owned_rank = jnp.cumsum(owned_mask) - 1
    picker = (owned_mask[None, :] == 1) & (
        owned_rank[None, :] == jnp.arange(BPD, dtype=jnp.int32)[:, None]
    )
    block_numbers = jnp.arange(owners.shape[0], dtype=jnp.int32)
    owned_blocks = jnp.sum(jnp.where(picker, block_numbers[None, :], 0), axis=1)
    sources = owned_blocks // BPD
    destination = lax.dynamic_slice_in_dim(owners, self_index * BPD, BPD, 0)
    block_starts = self_index * token_count + jnp.arange(BPD, dtype=jnp.int32) * block_len
    grad_query, attn_out, key_part, value_part = attention_backward(
        queries, attn_grad, block_starts, key_all, value_all, ends_row, block_len, key_block
    )
    outgoing = slot_buffer(
        grad_query.reshape(BPD, block_len, grad_query.shape[1]), destination, peer_count
    )
    incoming = lax.all_to_all(outgoing, "ctx", split_axis=0, concat_axis=0, tiled=True)
    grad_queries = compact_slots(incoming, sources, peer_count).reshape(
        token_count, grad_query.shape[1]
    )
    query_term = jnp.einsum("tr,tc->rc", input_proj, grad_query, preferred_element_type=jnp.float32)
    out_term = jnp.einsum("tr,tc->rc", grad_proj, attn_out, preferred_element_type=jnp.float32)
    key_sums, value_sums = (
        lax.psum_scatter(key_part, "ctx", scatter_dimension=0, tiled=True),
        lax.psum_scatter(value_part, "ctx", scatter_dimension=0, tiled=True),
    )
    grad_keys = key_sums.astype(jnp.bfloat16)
    grad_values = value_sums.astype(jnp.bfloat16)
    norm_factor = 1.0 / math.sqrt(token_count * peer_count * lax.axis_size("dp"))
    qkv_term = (
        jnp.concatenate(
            [
                query_term,
                jnp.einsum("tr,tc->rc", input_proj, grad_keys, preferred_element_type=jnp.float32),
                jnp.einsum(
                    "tr,tc->rc", input_proj, grad_values, preferred_element_type=jnp.float32
                ),
            ],
            axis=1,
        )
        * norm_factor
    )
    galore_qkv, galore_out = (
        lax.psum_scatter(qkv_term, ("dp", "ctx"), scatter_dimension=0, tiled=True),
        lax.psum_scatter(out_term * norm_factor, ("dp", "ctx"), scatter_dimension=0, tiled=True),
    )
    return (grad_queries, grad_keys, grad_values, galore_qkv, galore_out)


MESH = pl.DeviceIdType.MESH
CHUNKS = 4


def fused_kernel(
    dp_size,
    scale_out,
    lengths_ref,
    owner_ref,
    x_hbm,
    g_hbm,
    bq_hbm,
    bo_hbm,
    q_ref,
    k_ref,
    v_ref,
    do_ref,
    gq_out,
    gk_out,
    gv_out,
    gqkv_out,
    gout_out,
    xbuf,
    bbuf,
    kbuf,
    vbuf,
    bias,
    dkv,
    dkv_in,
    act,
    act_in,
    slots,
    gq_in,
    acc,
    tbuf,
    r1,
    s1,
    r2,
    fin,
    fin_in,
    lsem,
    kv_s,
    kv_r,
    x_s,
    x_r,
    b_s,
    b_r,
    dkv_s,
    dkv_r,
    gq_s,
    gq_r,
    act_s,
    act_r,
    t_s,
    t_r,
    z_s,
    z_r,
    f_s,
    f_r,
):
    dp = lax.axis_index("dp")
    me = lax.axis_index("ctx")
    core = lax.rem(dp, 2)
    z = dp // 2
    nz = dp_size // 2
    sib = dp + 1 - 2 * core
    peers = (me, me + 1 - 2 * lax.rem(me, 2), lax.rem(me + 2, 4), 3 - me)
    zpeers = [lax.rem(z + k, nz) for k in range(nz)]
    tokens = q_ref.shape[0]
    window = 4 * tokens
    depth = bq_hbm.shape[0]
    step = depth // CHUNKS
    blk = tokens // BPD
    f32, bf16 = jnp.float32, jnp.bfloat16

    def remote(src, dst, send, recv, dev):
        return pltpu.make_async_remote_copy(
            src_ref=src, dst_ref=dst, send_sem=send, recv_sem=recv, device_id=dev, device_id_type=MESH
        )

    own_x0 = pltpu.make_async_copy(x_hbm, xbuf.at[0], lsem.at[0])
    own_x1 = pltpu.make_async_copy(g_hbm, xbuf.at[0], lsem.at[0])
    own_b0 = pltpu.make_async_copy(bq_hbm, bbuf.at[0], lsem.at[1])
    own_b1 = pltpu.make_async_copy(bo_hbm, bbuf.at[0], lsem.at[1])

    @pl.when(core == 0)
    def _():
        own_b0.start()
        own_x0.start()

    @pl.when(core == 1)
    def _():
        own_b1.start()
        own_x1.start()

    barrier = pltpu.get_barrier_semaphore()
    for r in (1, 2, 3):
        pl.semaphore_signal(barrier, inc=1, device_id=(dp, peers[r]), device_id_type=MESH)
    pl.semaphore_signal(barrier, inc=1, device_id=(sib, me), device_id_type=MESH)
    for k in range(1, nz):
        pl.semaphore_signal(
            barrier, inc=1, device_id=(2 * zpeers[k] + core, me), device_id_type=MESH
        )
    pl.semaphore_wait(barrier, 3 + 1 + nz - 1)

    kv_copies = []
    for r in (1, 2, 3):
        for i, (src, dst) in enumerate(((k_ref, kbuf), (v_ref, vbuf))):
            n = 2 * (r - 1) + i
            kv_copies.append(
                remote(src, dst.at[me], kv_s.at[n], kv_r.at[n], (dp, peers[r]))
            )
    for c in kv_copies:
        c.start()

    own_b0.wait()

    def rows(chunk):
        return pl.ds(chunk * step, step)

    def basis_copy(slot, chunk, to, via, n):
        m = (to - 1) * CHUNKS + chunk
        return remote(
            bbuf.at[slot, rows(chunk)], bbuf.at[to, rows(chunk)], b_s.at[n], b_r.at[m], (dp, peers[via])
        )

    half = CHUNKS // 2
    to_x = [basis_copy(0, c, 1, 1, c) for c in range(CHUNKS)]
    to_y = [basis_copy(0, c, 2, 2, CHUNKS + c) for c in range(CHUNKS)]
    fwd = [
        basis_copy(1, c, 3, 2, 2 * CHUNKS + c)
        if c < half
        else basis_copy(2, c, 3, 1, 2 * CHUNKS + c)
        for c in range(CHUNKS)
    ]
    for i in range(CHUNKS):
        to_x[i].start()
        to_y[(i + half) % CHUNKS].start()

    sib_x0 = remote(g_hbm, xbuf.at[1], x_s, x_r, (sib, me))
    sib_x1 = remote(x_hbm, xbuf.at[1], x_s, x_r, (sib, me))

    @pl.when(core == 0)
    def _():
        sib_x0.start()

    @pl.when(core == 1)
    def _():
        sib_x1.start()

    kbuf[me] = k_ref[...]
    vbuf[me] = v_ref[...]
    pos = me * tokens + lax.broadcasted_iota(jnp.int32, (tokens, 1), 0)
    begin = jnp.zeros((tokens, 1), jnp.int32)
    end = jnp.int32(0)
    for n in range(lengths_ref.shape[1]):
        end = end + lengths_ref[0, n]
        begin = jnp.where(pos >= end, end, begin)
    key_pos = lax.broadcasted_iota(jnp.int32, (tokens, window), 1)
    bias[...] = jnp.where((key_pos <= pos) & (key_pos >= begin), 0.0, NEG_LARGE).astype(f32)
    dkv[...] = jnp.zeros_like(dkv)
    act[...] = jnp.zeros_like(act)

    for c in kv_copies:
        c.wait()

    scale = HD ** (-0.5)
    across = (((1,), (1,)), ((), ()))
    down = (((0,), (0,)), ((), ()))

    def head(h, carry):
        cols = pl.ds(pl.multiple_of(h * HD, HD), HD)
        key = kbuf[...].reshape(window, HD)
        val = vbuf[...].reshape(window, HD)
        q = q_ref[:, cols]
        do = do_ref[:, cols]
        s = lax.dot_general(q, key, across, preferred_element_type=f32) * scale + bias[...]
        top = jnp.max(s, axis=1, keepdims=True)
        e = jnp.exp(s - top)
        p = e * (1.0 / jnp.sum(e, axis=1, keepdims=True))
        w = p.astype(bf16)
        o = jnp.dot(w, val, preferred_element_type=f32).astype(bf16)
        delta = jnp.sum(do.astype(f32) * o.astype(f32), axis=1, keepdims=True)
        dprob = lax.dot_general(do, val, across, preferred_element_type=f32)
        ds = (p * (dprob - delta) * scale).astype(bf16)
        act[0, :, cols] = jnp.dot(ds, key, preferred_element_type=f32).astype(bf16)
        act[1, :, cols] = o
        dk = lax.dot_general(ds, q, down, preferred_element_type=f32)
        dv = lax.dot_general(w, do, down, preferred_element_type=f32)
        dkv[0] += dk.reshape(4, tokens, HD)
        dkv[1] += dv.reshape(4, tokens, HD)
        return carry

    lax.fori_loop(0, HQ, head, 0)

    dkv_copies = [
        remote(dkv.at[:, peers[r]], dkv_in.at[r - 1], dkv_s.at[r - 1], dkv_r.at[r - 1], (dp, peers[r]))
        for r in (1, 2, 3)
    ]
    for c in dkv_copies:
        c.start()

    wide = HQ * HD
    for d in range(4):
        chosen = jnp.zeros((blk, wide), f32)
        for j in range(BPD):
            piece = act[0, j * blk : (j + 1) * blk, :wide].astype(f32)
            chosen = jnp.where(owner_ref[0, me * BPD + j] == d, piece, chosen)
        slots[d] = chosen.astype(bf16)
    gq_copies = [
        remote(slots.at[peers[r]], gq_in.at[me], gq_s.at[r - 1], gq_r.at[r - 1], (dp, peers[r]))
        for r in (1, 2, 3)
    ]
    for c in gq_copies:
        c.start()
    gq_in[me] = slots[me]

    for c in dkv_copies:
        c.wait()
    for i, out in enumerate((gk_out, gv_out)):
        total = dkv[i, me] + dkv_in[0, i] + dkv_in[1, i] + dkv_in[2, i]
        total = total.astype(bf16)
        out[...] = total
        act[0, :, wide + i * HD : wide + (i + 1) * HD] = total
    act_copy = remote(act.at[1 - core], act_in, act_s, act_r, (sib, me))
    act_copy.start()

    own_x0.wait()
    sib_x0.wait()

    def add(slot, chunk, first=False):
        at = pl.multiple_of(peers[slot] * depth + chunk * step, step)
        x = xbuf[:, :, pl.ds(at, step)].reshape(2 * tokens, step)
        part = jnp.dot(x, bbuf[slot, chunk * step : (chunk + 1) * step, :], preferred_element_type=f32)
        if first:
            acc[...] = part
        else:
            acc[...] += part

    for c in range(CHUNKS):
        add(0, c, c == 0)
    for i in range(CHUNKS):
        j = (i + half) % CHUNKS
        to_x[i].wait_recv()
        if i < half:
            fwd[i].start()
        to_y[j].wait_recv()
        if j >= half:
            fwd[j].start()
        add(1, i)
        add(2, j)
    act_copy.wait()
    for c in gq_copies:
        c.wait()
    for d in range(4):
        gq_out[d * blk : (d + 1) * blk, :] = gq_in[d]
    for i in range(half):
        fwd[i].wait_recv()
        add(3, i)
        fwd[i + half].wait_recv()
        add(3, i + half)

    own_rows = acc.shape[1] // (dp_size * 4)
    per_dp = 4 * own_rows
    for d in range(dp_size):
        left = acc[:, (d // 2) * 2 * per_dp : (d // 2 + 1) * 2 * per_dp].astype(bf16)
        if d % 2 == 0:
            both = lax.dot_general(
                left[:tokens], act[core], down, preferred_element_type=f32
            ) + lax.dot_general(left[tokens:], act_in[...], down, preferred_element_type=f32)
            tbuf[d : d + 2] = both.astype(bf16).reshape(2, 4, own_rows, both.shape[1])
    t_copies = [
        remote(tbuf.at[:, peers[r]], r1.at[r - 1], t_s.at[r - 1], t_r.at[r - 1], (dp, peers[r]))
        for r in (1, 2, 3)
    ]
    for r in (2, 0, 1):
        t_copies[r].start()
    for c in to_x + to_y + fwd:
        c.wait_send()
    for c in t_copies:
        c.wait()
    for d in range(dp_size):
        total = tbuf[d, me].astype(f32) + r1[0, d].astype(f32)
        total = total + (r1[1, d].astype(f32) + r1[2, d].astype(f32))
        s1[d // 2, d % 2] = total.astype(bf16)
    z_copies = [
        remote(
            s1.at[zpeers[k]], r2.at[k - 1], z_s.at[k - 1], z_r.at[k - 1], (2 * zpeers[k] + core, me)
        )
        for k in range(1, nz)
    ]
    for c in z_copies:
        c.start()
    for c in z_copies:
        c.wait()
    total = s1[z].astype(f32)
    for k in range(1, nz):
        total = total + r2[k - 1].astype(f32)
    fin[...] = total * scale_out
    f_copy = remote(fin.at[1 - core], fin_in, f_s, f_r, (sib, me))
    f_copy.start()
    f_copy.wait()
    mine = fin[core]
    other = fin_in[...]
    gqkv_out[...] = jnp.where(core == 0, mine, other)
    gout_out[...] = jnp.where(core == 0, other, mine)[:, :wide]


def fused_shards(
    inputs,
    out_grad,
    queries,
    keys,
    values,
    attn_grad,
    doc_lengths,
    block_owner,
    basis_qkv,
    basis_out,
):
    dp_size = lax.axis_size("dp")
    nz = dp_size // 2
    tokens, width = inputs.shape
    depth, rank = basis_qkv.shape
    wide = queries.shape[1]
    cols = wide + 2 * HD
    own_rows = rank // (dp_size * 4)
    blk = tokens // BPD
    f32, bf16 = jnp.float32, jnp.bfloat16
    norm_factor = 1.0 / math.sqrt(tokens * 4 * dp_size)
    vmem = pl.BlockSpec(memory_space=pltpu.VMEM)
    smem = pl.BlockSpec(memory_space=pltpu.SMEM)
    hbm = pl.BlockSpec(memory_space=pl.ANY)
    dma = pltpu.SemaphoreType.DMA
    return pl.pallas_call(
        functools.partial(fused_kernel, dp_size, norm_factor),
        out_shape=(
            jax.ShapeDtypeStruct((tokens, wide), bf16),
            jax.ShapeDtypeStruct((tokens, HD), bf16),
            jax.ShapeDtypeStruct((tokens, HD), bf16),
            jax.ShapeDtypeStruct((own_rows, cols), f32),
            jax.ShapeDtypeStruct((own_rows, wide), f32),
        ),
        in_specs=[smem, smem, hbm, hbm, hbm, hbm, vmem, vmem, vmem, vmem],
        out_specs=[vmem] * 5,
        scratch_shapes=[
            pltpu.VMEM((2, tokens, width), bf16),
            pltpu.VMEM((4, depth, rank), bf16),
            pltpu.VMEM((4, tokens, HD), bf16),
            pltpu.VMEM((4, tokens, HD), bf16),
            pltpu.VMEM((tokens, 4 * tokens), f32),
            pltpu.VMEM((2, 4, tokens, HD), f32),
            pltpu.VMEM((3, 2, tokens, HD), f32),
            pltpu.VMEM((2, tokens, cols), bf16),
            pltpu.VMEM((tokens, cols), bf16),
            pltpu.VMEM((4, blk, wide), bf16),
            pltpu.VMEM((4, blk, wide), bf16),
            pltpu.VMEM((2 * tokens, rank), f32),
            pltpu.VMEM((dp_size, 4, own_rows, cols), bf16),
            pltpu.VMEM((3, dp_size, own_rows, cols), bf16),
            pltpu.VMEM((nz, 2, own_rows, cols), bf16),
            pltpu.VMEM((nz - 1, 2, own_rows, cols), bf16),
            pltpu.VMEM((2, own_rows, cols), f32),
            pltpu.VMEM((own_rows, cols), f32),
            dma((2,)),
            dma((6,)),
            dma((6,)),
            dma,
            dma,
            dma((3 * CHUNKS,)),
            dma((3 * CHUNKS,)),
            dma((3,)),
            dma((3,)),
            dma((3,)),
            dma((3,)),
            dma,
            dma,
            dma((3,)),
            dma((3,)),
            dma((nz - 1,)),
            dma((nz - 1,)),
            dma,
            dma,
        ],
        compiler_params=pltpu.CompilerParams(
            collective_id=0, has_side_effects=True, vmem_limit_bytes=48 * 1024 * 1024
        ),
        name="fused",
    )(
        doc_lengths,
        block_owner,
        inputs,
        out_grad,
        basis_qkv,
        basis_out,
        queries,
        keys,
        values,
        attn_grad,
    )


def solution(mesh):
    in_specs = (
        P(("dp", "ctx"), None),
        P(("dp", "ctx"), None),
        P(("dp", "ctx"), None),
        P(("dp", "ctx"), None),
        P(("dp", "ctx"), None),
        P(("dp", "ctx"), None),
        P("dp", None),
        P("dp", None),
        P("ctx", None),
        P("ctx", None),
    )
    out_specs = (
        P(("dp", "ctx"), None),
        P(("dp", "ctx"), None),
        P(("dp", "ctx"), None),
        P(("dp", "ctx"), None),
        P(("dp", "ctx"), None),
    )
    body = fused_shards if mesh.shape["ctx"] == 4 and mesh.shape["dp"] == 8 else shards
    return jax.shard_map(body, mesh=mesh, in_specs=in_specs, out_specs=out_specs, check_vma=False)
```

```python
import functools
import math

import jax
import jax.numpy as jnp
from jax import lax
from jax.experimental import pallas as pl
from jax.experimental.pallas import tpu as pltpu
from jax.sharding import PartitionSpec as P

HD = 128
HQ = 8
GROUPS = 1
BPD = 4


NEG_LARGE = -1e30


def doc_index_of(ends_row, positions):
    return jnp.sum((positions[:, None] >= ends_row[None, :]).astype(jnp.int32), axis=1)


def doc_start_of(ends_row, position):
    return jnp.max(jnp.where(ends_row <= position, ends_row, 0))


def slot_buffer(blocks, destination, peer_count):
    chooser = (destination[None, :] == jnp.arange(peer_count, dtype=jnp.int32)[:, None]).astype(
        blocks.dtype
    )
    return jnp.einsum("dj,jbf->dbf", chooser, blocks)


def compact_slots(received, sources, peer_count):
    chooser = (sources[:, None] == jnp.arange(peer_count, dtype=jnp.int32)[None, :]).astype(
        received.dtype
    )
    return jnp.einsum("kd,dbf->kbf", chooser, received)


def attend_group(
    query_rows,
    dout_rows,
    row_pos,
    row_docs,
    low_key,
    high_key,
    key_group,
    value_group,
    key_docs,
    key_block,
    grad_key,
    grad_value,
):
    scale_factor = HD ** (-0.5)
    block_count = key_group.shape[0] // key_block
    row_count = query_rows.shape[0]
    across = (((1,), (1,)), ((), ()))
    downward = (((0,), (0,)), ((), ()))

    def block_scores(block_id):
        begin_key = block_id * key_block
        key_piece = lax.dynamic_slice_in_dim(key_group, begin_key, key_block, 0)
        value_piece = lax.dynamic_slice_in_dim(value_group, begin_key, key_block, 0)
        piece_docs = lax.dynamic_slice_in_dim(key_docs, begin_key, key_block, 0)
        key_pos = begin_key + jnp.arange(key_block, dtype=jnp.int32)
        allowed = (row_docs[:, None] == piece_docs[None, :]) & (
            key_pos[None, :] <= row_pos[:, None]
        )
        scores = (
            lax.dot_general(query_rows, key_piece, across, preferred_element_type=jnp.float32)
            * scale_factor
        )
        return (scores, allowed, key_piece, value_piece)

    def needed(block_id):
        return (block_id * key_block <= high_key) & ((block_id + 1) * key_block > low_key)

    def stats_step(block_id, running):

        def stats_compute(stats_in):
            peak_old, total_old = stats_in
            scores, allowed, key_piece, value_piece = block_scores(block_id)
            peak_new = jnp.maximum(peak_old, jnp.max(jnp.where(allowed, scores, NEG_LARGE), axis=1))
            shifted = jnp.where(allowed, jnp.exp(scores - peak_new[:, None]), 0.0)
            return (peak_new, total_old * jnp.exp(peak_old - peak_new) + jnp.sum(shifted, axis=1))

        return lax.cond(needed(block_id), stats_compute, lambda unchanged: unchanged, running)

    start_stats = (
        jnp.full((row_count,), NEG_LARGE, jnp.float32),
        jnp.zeros((row_count,), jnp.float32),
    )
    peak_score, denom_total = lax.fori_loop(0, block_count, stats_step, start_stats)
    log_total = peak_score + jnp.log(denom_total)

    def out_step(block_id, running):

        def out_compute(acc_in):
            scores, allowed, key_piece, value_piece = block_scores(block_id)
            weights = jnp.where(allowed, jnp.exp(scores - log_total[:, None]), 0.0).astype(
                jnp.bfloat16
            )
            return acc_in + jnp.dot(weights, value_piece, preferred_element_type=jnp.float32)

        return lax.cond(needed(block_id), out_compute, lambda unchanged: unchanged, running)

    out_sums = lax.fori_loop(0, block_count, out_step, jnp.zeros((row_count, HD), jnp.float32))
    out_rows = out_sums.astype(jnp.bfloat16)
    row_delta = jnp.sum(dout_rows.astype(jnp.float32) * out_rows.astype(jnp.float32), axis=1)

    def grad_step(block_id, running):

        def grad_compute(carried):
            grad_query, key_acc, value_acc = carried
            scores, allowed, key_piece, value_piece = block_scores(block_id)
            probability = jnp.where(allowed, jnp.exp(scores - log_total[:, None]), 0.0)
            weights = probability.astype(jnp.bfloat16)
            grad_prob = lax.dot_general(
                dout_rows, value_piece, across, preferred_element_type=jnp.float32
            )
            grad_scores = (probability * (grad_prob - row_delta[:, None]) * scale_factor).astype(
                jnp.bfloat16
            )
            grad_query = grad_query + jnp.dot(
                grad_scores, key_piece, preferred_element_type=jnp.float32
            )
            begin_key = block_id * key_block
            key_update = lax.dot_general(
                grad_scores, query_rows, downward, preferred_element_type=jnp.float32
            )
            value_update = lax.dot_general(
                weights, dout_rows, downward, preferred_element_type=jnp.float32
            )
            key_acc = lax.dynamic_update_slice_in_dim(
                key_acc,
                lax.dynamic_slice_in_dim(key_acc, begin_key, key_block, 0) + key_update,
                begin_key,
                0,
            )
            value_acc = lax.dynamic_update_slice_in_dim(
                value_acc,
                lax.dynamic_slice_in_dim(value_acc, begin_key, key_block, 0) + value_update,
                begin_key,
                0,
            )
            return (grad_query, key_acc, value_acc)

        return lax.cond(needed(block_id), grad_compute, lambda unchanged: unchanged, running)

    start_grads = (jnp.zeros((row_count, HD), jnp.float32), grad_key, grad_value)
    grad_query, grad_key, grad_value = lax.fori_loop(0, block_count, grad_step, start_grads)
    return (grad_query.astype(jnp.bfloat16), out_rows, grad_key, grad_value)


def attention_backward(
    query_local, dout_local, block_starts, key_all, value_all, ends_row, block_len, key_block
):
    token_count = query_local.shape[0]
    window_len = key_all.shape[0]
    key_docs = doc_index_of(ends_row, jnp.arange(window_len, dtype=jnp.int32))
    query_view = query_local.reshape(token_count, GROUPS, HQ * HD)
    dout_view = dout_local.reshape(token_count, GROUPS, HQ * HD)
    query_groups, out_groups, key_groups, value_groups = ([], [], [], [])
    grad_key = jnp.zeros((window_len, HD), jnp.float32)
    grad_value = jnp.zeros((window_len, HD), jnp.float32)
    query_blocks = []
    out_blocks = []
    for block_id in range(BPD):
        first_pos = block_starts[block_id]
        lower_row = block_id * block_len
        query_rows = query_view[lower_row : lower_row + block_len, 0].reshape(block_len * HQ, HD)
        dout_rows = dout_view[lower_row : lower_row + block_len, 0].reshape(block_len * HQ, HD)
        row_pos = jnp.repeat(first_pos + jnp.arange(block_len, dtype=jnp.int32), HQ)
        row_docs = doc_index_of(ends_row, row_pos)
        low_key = doc_start_of(ends_row, first_pos)
        high_key = first_pos + block_len - 1
        grad_rows, out_rows, grad_key, grad_value = attend_group(
            query_rows,
            dout_rows,
            row_pos,
            row_docs,
            low_key,
            high_key,
            key_all,
            value_all,
            key_docs,
            key_block,
            grad_key,
            grad_value,
        )
        query_blocks.append(grad_rows.reshape(block_len, HQ * HD))
        out_blocks.append(out_rows.reshape(block_len, HQ * HD))
    query_groups.append(jnp.concatenate(query_blocks, axis=0))
    out_groups.append(jnp.concatenate(out_blocks, axis=0))
    key_groups.append(grad_key)
    value_groups.append(grad_value)
    return (query_groups[0], out_groups[0], key_groups[0], value_groups[0])


def shards(
    inputs,
    out_grad,
    queries,
    keys,
    values,
    attn_grad,
    doc_lengths,
    block_owner,
    basis_qkv,
    basis_out,
):
    peer_count = lax.axis_size("ctx")
    self_index = lax.axis_index("ctx")
    token_count = inputs.shape[0]
    window_len = token_count * peer_count
    block_len = token_count // BPD
    key_block = min(512, window_len)
    ends_row = jnp.cumsum(doc_lengths[0])
    owners = block_owner[0]
    input_sums = jnp.dot(
        inputs,
        lax.all_gather(basis_qkv, "ctx", axis=0, tiled=True),
        preferred_element_type=jnp.float32,
    )
    grad_sums = jnp.dot(
        out_grad,
        lax.all_gather(basis_out, "ctx", axis=0, tiled=True),
        preferred_element_type=jnp.float32,
    )
    input_proj = input_sums.astype(jnp.bfloat16)
    grad_proj = grad_sums.astype(jnp.bfloat16)
    key_all, value_all = (
        lax.all_gather(keys, "ctx", axis=0, tiled=True),
        lax.all_gather(values, "ctx", axis=0, tiled=True),
    )
    owned_mask = (owners == self_index).astype(jnp.int32)
    owned_rank = jnp.cumsum(owned_mask) - 1
    picker = (owned_mask[None, :] == 1) & (
        owned_rank[None, :] == jnp.arange(BPD, dtype=jnp.int32)[:, None]
    )
    block_numbers = jnp.arange(owners.shape[0], dtype=jnp.int32)
    owned_blocks = jnp.sum(jnp.where(picker, block_numbers[None, :], 0), axis=1)
    sources = owned_blocks // BPD
    destination = lax.dynamic_slice_in_dim(owners, self_index * BPD, BPD, 0)
    block_starts = self_index * token_count + jnp.arange(BPD, dtype=jnp.int32) * block_len
    grad_query, attn_out, key_part, value_part = attention_backward(
        queries, attn_grad, block_starts, key_all, value_all, ends_row, block_len, key_block
    )
    outgoing = slot_buffer(
        grad_query.reshape(BPD, block_len, grad_query.shape[1]), destination, peer_count
    )
    incoming = lax.all_to_all(outgoing, "ctx", split_axis=0, concat_axis=0, tiled=True)
    grad_queries = compact_slots(incoming, sources, peer_count).reshape(
        token_count, grad_query.shape[1]
    )
    query_term = jnp.einsum("tr,tc->rc", input_proj, grad_query, preferred_element_type=jnp.float32)
    out_term = jnp.einsum("tr,tc->rc", grad_proj, attn_out, preferred_element_type=jnp.float32)
    key_sums, value_sums = (
        lax.psum_scatter(key_part, "ctx", scatter_dimension=0, tiled=True),
        lax.psum_scatter(value_part, "ctx", scatter_dimension=0, tiled=True),
    )
    grad_keys = key_sums.astype(jnp.bfloat16)
    grad_values = value_sums.astype(jnp.bfloat16)
    norm_factor = 1.0 / math.sqrt(token_count * peer_count * lax.axis_size("dp"))
    qkv_term = (
        jnp.concatenate(
            [
                query_term,
                jnp.einsum("tr,tc->rc", input_proj, grad_keys, preferred_element_type=jnp.float32),
                jnp.einsum(
                    "tr,tc->rc", input_proj, grad_values, preferred_element_type=jnp.float32
                ),
            ],
            axis=1,
        )
        * norm_factor
    )
    galore_qkv, galore_out = (
        lax.psum_scatter(qkv_term, ("dp", "ctx"), scatter_dimension=0, tiled=True),
        lax.psum_scatter(out_term * norm_factor, ("dp", "ctx"), scatter_dimension=0, tiled=True),
    )
    return (grad_queries, grad_keys, grad_values, galore_qkv, galore_out)


MESH = pl.DeviceIdType.MESH
CHUNKS = 8


def fused_kernel(
    dp_size,
    scale_out,
    lengths_hbm,
    owner_hbm,
    x_hbm,
    g_hbm,
    bq_hbm,
    bo_hbm,
    q_hbm,
    k_hbm,
    v_hbm,
    do_hbm,
    gq_out,
    gk_out,
    gv_out,
    gqkv_out,
    gout_out,
    lengths_ref,
    owner_ref,
    q_ref,
    do_ref,
    xbuf,
    bbuf,
    kbuf,
    vbuf,
    bias,
    dkv,
    dkv_in,
    act,
    act_in,
    slots,
    gq_in,
    acc,
    tbuf,
    r1,
    s1,
    r2,
    fin,
    fin_in,
    lsem,
    kv_s,
    kv_r,
    x_s,
    x_r,
    b_s,
    b_r,
    dkv_s,
    dkv_r,
    gq_s,
    gq_r,
    act_s,
    act_r,
    t_s,
    t_r,
    z_s,
    z_r,
    f_s,
    f_r,
):
    dp = lax.axis_index("dp")
    me = lax.axis_index("ctx")
    core = lax.rem(dp, 2)
    z = dp // 2
    nz = dp_size // 2
    sib = dp + 1 - 2 * core
    peers = (me, me + 1 - 2 * lax.rem(me, 2), lax.rem(me + 2, 4), 3 - me)
    zpeers = [lax.rem(z + k, nz) for k in range(nz)]
    tokens = q_ref.shape[0]
    window = 4 * tokens
    depth = bq_hbm.shape[0]
    step = depth // CHUNKS
    blk = tokens // BPD
    f32, bf16 = jnp.float32, jnp.bfloat16

    def remote(src, dst, send, recv, dev):
        return pltpu.make_async_remote_copy(
            src_ref=src, dst_ref=dst, send_sem=send, recv_sem=recv, device_id=dev, device_id_type=MESH
        )

    own_x0 = pltpu.make_async_copy(x_hbm, xbuf.at[0], lsem.at[0])
    own_x1 = pltpu.make_async_copy(g_hbm, xbuf.at[0], lsem.at[0])
    own_b0 = pltpu.make_async_copy(bq_hbm, bbuf.at[0], lsem.at[1])
    own_b1 = pltpu.make_async_copy(bo_hbm, bbuf.at[0], lsem.at[1])

    @pl.when(core == 0)
    def _():
        own_b0.start()
        own_x0.start()

    @pl.when(core == 1)
    def _():
        own_b1.start()
        own_x1.start()

    small = [
        pltpu.make_async_copy(src, dst, lsem.at[2 + n])
        for n, (src, dst) in enumerate(
            (
                (lengths_hbm, lengths_ref),
                (owner_hbm, owner_ref),
                (q_hbm, q_ref),
                (do_hbm, do_ref),
                (k_hbm, kbuf.at[me]),
                (v_hbm, vbuf.at[me]),
            )
        )
    ]
    for c in small:
        c.start()
    barrier = pltpu.get_barrier_semaphore()
    for r in (1, 2, 3):
        pl.semaphore_signal(barrier, inc=1, device_id=(dp, peers[r]), device_id_type=MESH)
    pl.semaphore_signal(barrier, inc=1, device_id=(sib, me), device_id_type=MESH)
    zp = 2 * (z + 1 - 2 * lax.rem(z, 2)) + core
    for k in range(1, nz):
        pl.semaphore_signal(
            barrier, inc=1, device_id=(2 * zpeers[k] + core, me), device_id_type=MESH
        )
    pl.semaphore_wait(barrier, 3 + 1 + nz - 1)

    kv_copies = []
    for r in (1, 2, 3):
        for i, (src, dst) in enumerate(((k_hbm, kbuf), (v_hbm, vbuf))):
            n = 2 * (r - 1) + i
            kv_copies.append(
                remote(src, dst.at[me], kv_s.at[n], kv_r.at[n], (dp, peers[r]))
            )
    for c in kv_copies:
        c.start()

    own_b0.wait()

    par = lax.rem(z, 2)

    def spot(k):
        return k + par * (CHUNKS - 1 - 2 * k)

    def rows(k):
        return pl.ds(pl.multiple_of(spot(k) * step, step), step)

    unit = CHUNKS // 4
    count = [0]

    def basis_copy(slot, k, to, dev):
        n = count[0]
        count[0] += 1
        m = (to - 1) * CHUNKS + spot(k)
        return remote(
            bbuf.at[slot, rows(k)], bbuf.at[to, rows(k)], b_s.at[n], b_r.at[m], dev
        )

    def arrived(slot, k):
        m = (slot - 1) * CHUNKS + spot(k)
        remote(
            bbuf.at[0, rows(k)], bbuf.at[slot, rows(k)], b_s.at[0], b_r.at[m], x_dev
        ).wait_recv()

    x_dev, y_dev, z_dev = (dp, peers[1]), (dp, peers[2]), (zp, me)
    groups = [list(range(g * unit, (g + 1) * unit)) for g in range(4)]
    early, late = [], []
    for k, j in zip(groups[0], groups[1]):
        early.append(basis_copy(0, k, 1, x_dev))
        early.append(basis_copy(0, j, 2, y_dev))
    for k, j in zip(groups[1] + groups[2], groups[0] + groups[3]):
        late.append(basis_copy(0, k, 1, x_dev))
        late.append(basis_copy(0, j, 2, y_dev))
    fwd_y = [basis_copy(1, k, 3, y_dev) for k in groups[0]]
    fwd_x = [basis_copy(2, k, 3, x_dev) for k in groups[1]]
    over_z1 = [basis_copy(1, k, 1, z_dev) for k in groups[0]]
    over_z2 = [basis_copy(2, k, 2, z_dev) for k in groups[1]]
    over_z3 = [basis_copy(3, k, 3, z_dev) for k in groups[0] + groups[1]]
    for c in early:
        c.start()

    sib_x0 = remote(g_hbm, xbuf.at[1], x_s, x_r, (sib, me))
    sib_x1 = remote(x_hbm, xbuf.at[1], x_s, x_r, (sib, me))

    @pl.when(core == 0)
    def _():
        sib_x0.start()

    @pl.when(core == 1)
    def _():
        sib_x1.start()

    for c in small:
        c.wait()
    pos = me * tokens + lax.broadcasted_iota(jnp.int32, (tokens, 1), 0)
    begin = jnp.zeros((tokens, 1), jnp.int32)
    end = jnp.int32(0)
    for n in range(lengths_ref.shape[1]):
        end = end + lengths_ref[0, n]
        begin = jnp.where(pos >= end, end, begin)
    key_pos = lax.broadcasted_iota(jnp.int32, (tokens, window), 1)
    bias[...] = jnp.where((key_pos <= pos) & (key_pos >= begin), 0.0, NEG_LARGE).astype(f32)
    dkv[...] = jnp.zeros_like(dkv)
    act[...] = jnp.zeros_like(act)

    for c in kv_copies:
        c.wait()

    scale = HD ** (-0.5)
    across = (((1,), (1,)), ((), ()))
    down = (((0,), (0,)), ((), ()))

    def head(h, carry):
        cols = pl.ds(pl.multiple_of(h * HD, HD), HD)
        key = kbuf[...].reshape(window, HD)
        val = vbuf[...].reshape(window, HD)
        q = q_ref[:, cols]
        do = do_ref[:, cols]
        s = lax.dot_general(q, key, across, preferred_element_type=f32) * scale + bias[...]
        top = jnp.max(s, axis=1, keepdims=True)
        e = jnp.exp(s - top)
        p = e * (1.0 / jnp.sum(e, axis=1, keepdims=True))
        w = p.astype(bf16)
        o = jnp.dot(w, val, preferred_element_type=f32).astype(bf16)
        delta = jnp.sum(do.astype(f32) * o.astype(f32), axis=1, keepdims=True)
        dprob = lax.dot_general(do, val, across, preferred_element_type=f32)
        ds = (p * (dprob - delta) * scale).astype(bf16)
        act[0, :, cols] = jnp.dot(ds, key, preferred_element_type=f32).astype(bf16)
        act[1, :, cols] = o
        dk = lax.dot_general(ds, q, down, preferred_element_type=f32)
        dv = lax.dot_general(w, do, down, preferred_element_type=f32)
        dkv[0] += dk.reshape(4, tokens, HD)
        dkv[1] += dv.reshape(4, tokens, HD)
        return carry

    lax.fori_loop(0, HQ, head, 0)

    for i in range(unit):
        arrived(1, groups[0][i])
        fwd_y[i].start()
        over_z1[i].start()
        arrived(2, groups[1][i])
        fwd_x[i].start()
        over_z2[i].start()

    dkv_copies = [
        remote(dkv.at[:, peers[r]], dkv_in.at[r - 1], dkv_s.at[r - 1], dkv_r.at[r - 1], (dp, peers[r]))
        for r in (1, 2, 3)
    ]
    for c in dkv_copies:
        c.start()

    wide = HQ * HD
    for d in range(4):
        chosen = jnp.zeros((blk, wide), f32)
        for j in range(BPD):
            piece = act[0, j * blk : (j + 1) * blk, :wide].astype(f32)
            chosen = jnp.where(owner_ref[0, me * BPD + j] == d, piece, chosen)
        slots[d] = chosen.astype(bf16)
    gq_copies = [
        remote(slots.at[peers[r]], gq_in.at[me], gq_s.at[r - 1], gq_r.at[r - 1], (dp, peers[r]))
        for r in (1, 2, 3)
    ]
    for c in gq_copies:
        c.start()
    gq_in[me] = slots[me]

    for c in dkv_copies:
        c.wait()
    for i, out in enumerate((gk_out, gv_out)):
        total = dkv[i, me] + dkv_in[0, i] + dkv_in[1, i] + dkv_in[2, i]
        total = total.astype(bf16)
        out[...] = total
        act[0, :, wide + i * HD : wide + (i + 1) * HD] = total
    act_copy = remote(act.at[1 - core], act_in, act_s, act_r, (sib, me))
    act_copy.start()

    own_x0.wait()
    sib_x0.wait()

    def add(slot, k, first=False):
        at = pl.multiple_of(peers[slot] * depth + spot(k) * step, step)
        x = xbuf[:, :, pl.ds(at, step)].reshape(2 * tokens, step)
        part = jnp.dot(x, bbuf[slot, rows(k), :], preferred_element_type=f32)
        if first:
            acc[...] = part
        else:
            acc[...] += part

    for i in range(unit):
        arrived(3, groups[0][i])
        over_z3[i].start()
        arrived(3, groups[1][i])
        over_z3[unit + i].start()
    for c in late:
        c.start()
    for k in range(CHUNKS):
        add(0, k, k == 0)
    for k in groups[0] + groups[1]:
        add(3, k)
    for k, j in zip(groups[0], groups[1]):
        add(1, k)
        add(2, j)
    for k, j in zip(groups[1], groups[0]):
        arrived(1, k)
        add(1, k)
        arrived(2, j)
        add(2, j)
    act_copy.wait()
    for c in gq_copies:
        c.wait()
    for d in range(4):
        gq_out[d * blk : (d + 1) * blk, :] = gq_in[d]
    for k, j in zip(groups[2], groups[3]):
        arrived(1, k)
        add(1, k)
        arrived(2, j)
        add(2, j)
    for k, j in zip(groups[3], groups[2]):
        arrived(1, k)
        add(1, k)
        arrived(2, j)
        add(2, j)
    for k in groups[3][::-1] + groups[2][::-1]:
        arrived(3, k)
        add(3, k)

    own_rows = acc.shape[1] // (dp_size * 4)
    per_dp = 4 * own_rows
    for d in range(dp_size):
        left = acc[:, (d // 2) * 2 * per_dp : (d // 2 + 1) * 2 * per_dp].astype(bf16)
        if d % 2 == 0:
            both = lax.dot_general(
                left[:tokens], act[core], down, preferred_element_type=f32
            ) + lax.dot_general(left[tokens:], act_in[...], down, preferred_element_type=f32)
            tbuf[d : d + 2] = both.astype(bf16).reshape(2, 4, own_rows, both.shape[1])
    t_copies = [
        remote(tbuf.at[:, peers[r]], r1.at[r - 1], t_s.at[r - 1], t_r.at[r - 1], (dp, peers[r]))
        for r in (1, 2, 3)
    ]
    for r in (2, 0, 1):
        t_copies[r].start()
    for c in early + late + fwd_x + fwd_y + over_z1 + over_z2 + over_z3:
        c.wait_send()
    for c in t_copies:
        c.wait()
    for d in range(dp_size):
        total = tbuf[d, me].astype(f32) + r1[0, d].astype(f32)
        total = total + (r1[1, d].astype(f32) + r1[2, d].astype(f32))
        s1[d // 2, d % 2] = total.astype(bf16)
    z_copies = [
        remote(
            s1.at[zpeers[k]], r2.at[k - 1], z_s.at[k - 1], z_r.at[k - 1], (2 * zpeers[k] + core, me)
        )
        for k in range(1, nz)
    ]
    for c in z_copies:
        c.start()
    for c in z_copies:
        c.wait()
    total = s1[z].astype(f32)
    for k in range(1, nz):
        total = total + r2[k - 1].astype(f32)
    fin[...] = total * scale_out
    f_copy = remote(fin.at[1 - core], fin_in, f_s, f_r, (sib, me))
    f_copy.start()
    f_copy.wait()
    mine = fin[core]
    other = fin_in[...]
    gqkv_out[...] = jnp.where(core == 0, mine, other)
    gout_out[...] = jnp.where(core == 0, other, mine)[:, :wide]


def fused_shards(
    inputs,
    out_grad,
    queries,
    keys,
    values,
    attn_grad,
    doc_lengths,
    block_owner,
    basis_qkv,
    basis_out,
):
    dp_size = lax.axis_size("dp")
    nz = dp_size // 2
    tokens, width = inputs.shape
    depth, rank = basis_qkv.shape
    wide = queries.shape[1]
    cols = wide + 2 * HD
    own_rows = rank // (dp_size * 4)
    blk = tokens // BPD
    f32, bf16 = jnp.float32, jnp.bfloat16
    norm_factor = 1.0 / math.sqrt(tokens * 4 * dp_size)
    vmem = pl.BlockSpec(memory_space=pltpu.VMEM)
    hbm = pl.BlockSpec(memory_space=pl.ANY)
    dma = pltpu.SemaphoreType.DMA
    return pl.pallas_call(
        functools.partial(fused_kernel, dp_size, norm_factor),
        out_shape=(
            jax.ShapeDtypeStruct((tokens, wide), bf16),
            jax.ShapeDtypeStruct((tokens, HD), bf16),
            jax.ShapeDtypeStruct((tokens, HD), bf16),
            jax.ShapeDtypeStruct((own_rows, cols), f32),
            jax.ShapeDtypeStruct((own_rows, wide), f32),
        ),
        in_specs=[hbm] * 10,
        out_specs=[vmem] * 5,
        scratch_shapes=[
            pltpu.SMEM(doc_lengths.shape, jnp.int32),
            pltpu.SMEM(block_owner.shape, jnp.int32),
            pltpu.VMEM((tokens, wide), bf16),
            pltpu.VMEM((tokens, wide), bf16),
            pltpu.VMEM((2, tokens, width), bf16),
            pltpu.VMEM((4, depth, rank), bf16),
            pltpu.VMEM((4, tokens, HD), bf16),
            pltpu.VMEM((4, tokens, HD), bf16),
            pltpu.VMEM((tokens, 4 * tokens), f32),
            pltpu.VMEM((2, 4, tokens, HD), f32),
            pltpu.VMEM((3, 2, tokens, HD), f32),
            pltpu.VMEM((2, tokens, cols), bf16),
            pltpu.VMEM((tokens, cols), bf16),
            pltpu.VMEM((4, blk, wide), bf16),
            pltpu.VMEM((4, blk, wide), bf16),
            pltpu.VMEM((2 * tokens, rank), f32),
            pltpu.VMEM((dp_size, 4, own_rows, cols), bf16),
            pltpu.VMEM((3, dp_size, own_rows, cols), bf16),
            pltpu.VMEM((nz, 2, own_rows, cols), bf16),
            pltpu.VMEM((nz - 1, 2, own_rows, cols), bf16),
            pltpu.VMEM((2, own_rows, cols), f32),
            pltpu.VMEM((own_rows, cols), f32),
            dma((8,)),
            dma((6,)),
            dma((6,)),
            dma,
            dma,
            dma((3 * CHUNKS,)),
            dma((3 * CHUNKS,)),
            dma((3,)),
            dma((3,)),
            dma((3,)),
            dma((3,)),
            dma,
            dma,
            dma((3,)),
            dma((3,)),
            dma((nz - 1,)),
            dma((nz - 1,)),
            dma,
            dma,
        ],
        compiler_params=pltpu.CompilerParams(
            collective_id=0, has_side_effects=True, vmem_limit_bytes=60 * 1024 * 1024
        ),
        name="fused",
    )(
        doc_lengths,
        block_owner,
        inputs,
        out_grad,
        basis_qkv,
        basis_out,
        queries,
        keys,
        values,
        attn_grad,
    )


def solution(mesh):
    in_specs = (
        P(("dp", "ctx"), None),
        P(("dp", "ctx"), None),
        P(("dp", "ctx"), None),
        P(("dp", "ctx"), None),
        P(("dp", "ctx"), None),
        P(("dp", "ctx"), None),
        P("dp", None),
        P("dp", None),
        P("ctx", None),
        P("ctx", None),
    )
    out_specs = (
        P(("dp", "ctx"), None),
        P(("dp", "ctx"), None),
        P(("dp", "ctx"), None),
        P(("dp", "ctx"), None),
        P(("dp", "ctx"), None),
    )
    body = fused_shards if mesh.shape["ctx"] == 4 and mesh.shape["dp"] == 8 else shards
    return jax.shard_map(body, mesh=mesh, in_specs=in_specs, out_specs=out_specs, check_vma=False)
```

```python
import functools
import math

import jax
import jax.numpy as jnp
from jax import lax
from jax.experimental import pallas as pl
from jax.experimental.pallas import tpu as pltpu
from jax.sharding import PartitionSpec as P

HD = 128
HQ = 8
GROUPS = 1
BPD = 4


NEG_LARGE = -1e30


def doc_index_of(ends_row, positions):
    return jnp.sum((positions[:, None] >= ends_row[None, :]).astype(jnp.int32), axis=1)


def doc_start_of(ends_row, position):
    return jnp.max(jnp.where(ends_row <= position, ends_row, 0))


def slot_buffer(blocks, destination, peer_count):
    chooser = (destination[None, :] == jnp.arange(peer_count, dtype=jnp.int32)[:, None]).astype(
        blocks.dtype
    )
    return jnp.einsum("dj,jbf->dbf", chooser, blocks)


def compact_slots(received, sources, peer_count):
    chooser = (sources[:, None] == jnp.arange(peer_count, dtype=jnp.int32)[None, :]).astype(
        received.dtype
    )
    return jnp.einsum("kd,dbf->kbf", chooser, received)


def attend_group(
    query_rows,
    dout_rows,
    row_pos,
    row_docs,
    low_key,
    high_key,
    key_group,
    value_group,
    key_docs,
    key_block,
    grad_key,
    grad_value,
):
    scale_factor = HD ** (-0.5)
    block_count = key_group.shape[0] // key_block
    row_count = query_rows.shape[0]
    across = (((1,), (1,)), ((), ()))
    downward = (((0,), (0,)), ((), ()))

    def block_scores(block_id):
        begin_key = block_id * key_block
        key_piece = lax.dynamic_slice_in_dim(key_group, begin_key, key_block, 0)
        value_piece = lax.dynamic_slice_in_dim(value_group, begin_key, key_block, 0)
        piece_docs = lax.dynamic_slice_in_dim(key_docs, begin_key, key_block, 0)
        key_pos = begin_key + jnp.arange(key_block, dtype=jnp.int32)
        allowed = (row_docs[:, None] == piece_docs[None, :]) & (
            key_pos[None, :] <= row_pos[:, None]
        )
        scores = (
            lax.dot_general(query_rows, key_piece, across, preferred_element_type=jnp.float32)
            * scale_factor
        )
        return (scores, allowed, key_piece, value_piece)

    def needed(block_id):
        return (block_id * key_block <= high_key) & ((block_id + 1) * key_block > low_key)

    def stats_step(block_id, running):

        def stats_compute(stats_in):
            peak_old, total_old = stats_in
            scores, allowed, key_piece, value_piece = block_scores(block_id)
            peak_new = jnp.maximum(peak_old, jnp.max(jnp.where(allowed, scores, NEG_LARGE), axis=1))
            shifted = jnp.where(allowed, jnp.exp(scores - peak_new[:, None]), 0.0)
            return (peak_new, total_old * jnp.exp(peak_old - peak_new) + jnp.sum(shifted, axis=1))

        return lax.cond(needed(block_id), stats_compute, lambda unchanged: unchanged, running)

    start_stats = (
        jnp.full((row_count,), NEG_LARGE, jnp.float32),
        jnp.zeros((row_count,), jnp.float32),
    )
    peak_score, denom_total = lax.fori_loop(0, block_count, stats_step, start_stats)
    log_total = peak_score + jnp.log(denom_total)

    def out_step(block_id, running):

        def out_compute(acc_in):
            scores, allowed, key_piece, value_piece = block_scores(block_id)
            weights = jnp.where(allowed, jnp.exp(scores - log_total[:, None]), 0.0).astype(
                jnp.bfloat16
            )
            return acc_in + jnp.dot(weights, value_piece, preferred_element_type=jnp.float32)

        return lax.cond(needed(block_id), out_compute, lambda unchanged: unchanged, running)

    out_sums = lax.fori_loop(0, block_count, out_step, jnp.zeros((row_count, HD), jnp.float32))
    out_rows = out_sums.astype(jnp.bfloat16)
    row_delta = jnp.sum(dout_rows.astype(jnp.float32) * out_rows.astype(jnp.float32), axis=1)

    def grad_step(block_id, running):

        def grad_compute(carried):
            grad_query, key_acc, value_acc = carried
            scores, allowed, key_piece, value_piece = block_scores(block_id)
            probability = jnp.where(allowed, jnp.exp(scores - log_total[:, None]), 0.0)
            weights = probability.astype(jnp.bfloat16)
            grad_prob = lax.dot_general(
                dout_rows, value_piece, across, preferred_element_type=jnp.float32
            )
            grad_scores = (probability * (grad_prob - row_delta[:, None]) * scale_factor).astype(
                jnp.bfloat16
            )
            grad_query = grad_query + jnp.dot(
                grad_scores, key_piece, preferred_element_type=jnp.float32
            )
            begin_key = block_id * key_block
            key_update = lax.dot_general(
                grad_scores, query_rows, downward, preferred_element_type=jnp.float32
            )
            value_update = lax.dot_general(
                weights, dout_rows, downward, preferred_element_type=jnp.float32
            )
            key_acc = lax.dynamic_update_slice_in_dim(
                key_acc,
                lax.dynamic_slice_in_dim(key_acc, begin_key, key_block, 0) + key_update,
                begin_key,
                0,
            )
            value_acc = lax.dynamic_update_slice_in_dim(
                value_acc,
                lax.dynamic_slice_in_dim(value_acc, begin_key, key_block, 0) + value_update,
                begin_key,
                0,
            )
            return (grad_query, key_acc, value_acc)

        return lax.cond(needed(block_id), grad_compute, lambda unchanged: unchanged, running)

    start_grads = (jnp.zeros((row_count, HD), jnp.float32), grad_key, grad_value)
    grad_query, grad_key, grad_value = lax.fori_loop(0, block_count, grad_step, start_grads)
    return (grad_query.astype(jnp.bfloat16), out_rows, grad_key, grad_value)


def attention_backward(
    query_local, dout_local, block_starts, key_all, value_all, ends_row, block_len, key_block
):
    token_count = query_local.shape[0]
    window_len = key_all.shape[0]
    key_docs = doc_index_of(ends_row, jnp.arange(window_len, dtype=jnp.int32))
    query_view = query_local.reshape(token_count, GROUPS, HQ * HD)
    dout_view = dout_local.reshape(token_count, GROUPS, HQ * HD)
    query_groups, out_groups, key_groups, value_groups = ([], [], [], [])
    grad_key = jnp.zeros((window_len, HD), jnp.float32)
    grad_value = jnp.zeros((window_len, HD), jnp.float32)
    query_blocks = []
    out_blocks = []
    for block_id in range(BPD):
        first_pos = block_starts[block_id]
        lower_row = block_id * block_len
        query_rows = query_view[lower_row : lower_row + block_len, 0].reshape(block_len * HQ, HD)
        dout_rows = dout_view[lower_row : lower_row + block_len, 0].reshape(block_len * HQ, HD)
        row_pos = jnp.repeat(first_pos + jnp.arange(block_len, dtype=jnp.int32), HQ)
        row_docs = doc_index_of(ends_row, row_pos)
        low_key = doc_start_of(ends_row, first_pos)
        high_key = first_pos + block_len - 1
        grad_rows, out_rows, grad_key, grad_value = attend_group(
            query_rows,
            dout_rows,
            row_pos,
            row_docs,
            low_key,
            high_key,
            key_all,
            value_all,
            key_docs,
            key_block,
            grad_key,
            grad_value,
        )
        query_blocks.append(grad_rows.reshape(block_len, HQ * HD))
        out_blocks.append(out_rows.reshape(block_len, HQ * HD))
    query_groups.append(jnp.concatenate(query_blocks, axis=0))
    out_groups.append(jnp.concatenate(out_blocks, axis=0))
    key_groups.append(grad_key)
    value_groups.append(grad_value)
    return (query_groups[0], out_groups[0], key_groups[0], value_groups[0])


def shards(
    inputs,
    out_grad,
    queries,
    keys,
    values,
    attn_grad,
    doc_lengths,
    block_owner,
    basis_qkv,
    basis_out,
):
    peer_count = lax.axis_size("ctx")
    self_index = lax.axis_index("ctx")
    token_count = inputs.shape[0]
    window_len = token_count * peer_count
    block_len = token_count // BPD
    key_block = min(512, window_len)
    ends_row = jnp.cumsum(doc_lengths[0])
    owners = block_owner[0]
    input_sums = jnp.dot(
        inputs,
        lax.all_gather(basis_qkv, "ctx", axis=0, tiled=True),
        preferred_element_type=jnp.float32,
    )
    grad_sums = jnp.dot(
        out_grad,
        lax.all_gather(basis_out, "ctx", axis=0, tiled=True),
        preferred_element_type=jnp.float32,
    )
    input_proj = input_sums.astype(jnp.bfloat16)
    grad_proj = grad_sums.astype(jnp.bfloat16)
    key_all, value_all = (
        lax.all_gather(keys, "ctx", axis=0, tiled=True),
        lax.all_gather(values, "ctx", axis=0, tiled=True),
    )
    owned_mask = (owners == self_index).astype(jnp.int32)
    owned_rank = jnp.cumsum(owned_mask) - 1
    picker = (owned_mask[None, :] == 1) & (
        owned_rank[None, :] == jnp.arange(BPD, dtype=jnp.int32)[:, None]
    )
    block_numbers = jnp.arange(owners.shape[0], dtype=jnp.int32)
    owned_blocks = jnp.sum(jnp.where(picker, block_numbers[None, :], 0), axis=1)
    sources = owned_blocks // BPD
    destination = lax.dynamic_slice_in_dim(owners, self_index * BPD, BPD, 0)
    block_starts = self_index * token_count + jnp.arange(BPD, dtype=jnp.int32) * block_len
    grad_query, attn_out, key_part, value_part = attention_backward(
        queries, attn_grad, block_starts, key_all, value_all, ends_row, block_len, key_block
    )
    outgoing = slot_buffer(
        grad_query.reshape(BPD, block_len, grad_query.shape[1]), destination, peer_count
    )
    incoming = lax.all_to_all(outgoing, "ctx", split_axis=0, concat_axis=0, tiled=True)
    grad_queries = compact_slots(incoming, sources, peer_count).reshape(
        token_count, grad_query.shape[1]
    )
    query_term = jnp.einsum("tr,tc->rc", input_proj, grad_query, preferred_element_type=jnp.float32)
    out_term = jnp.einsum("tr,tc->rc", grad_proj, attn_out, preferred_element_type=jnp.float32)
    key_sums, value_sums = (
        lax.psum_scatter(key_part, "ctx", scatter_dimension=0, tiled=True),
        lax.psum_scatter(value_part, "ctx", scatter_dimension=0, tiled=True),
    )
    grad_keys = key_sums.astype(jnp.bfloat16)
    grad_values = value_sums.astype(jnp.bfloat16)
    norm_factor = 1.0 / math.sqrt(token_count * peer_count * lax.axis_size("dp"))
    qkv_term = (
        jnp.concatenate(
            [
                query_term,
                jnp.einsum("tr,tc->rc", input_proj, grad_keys, preferred_element_type=jnp.float32),
                jnp.einsum(
                    "tr,tc->rc", input_proj, grad_values, preferred_element_type=jnp.float32
                ),
            ],
            axis=1,
        )
        * norm_factor
    )
    galore_qkv, galore_out = (
        lax.psum_scatter(qkv_term, ("dp", "ctx"), scatter_dimension=0, tiled=True),
        lax.psum_scatter(out_term * norm_factor, ("dp", "ctx"), scatter_dimension=0, tiled=True),
    )
    return (grad_queries, grad_keys, grad_values, galore_qkv, galore_out)


MESH = pl.DeviceIdType.MESH
CHUNKS = 8


def fused_kernel(
    dp_size,
    scale_out,
    lengths_hbm,
    owner_hbm,
    x_hbm,
    g_hbm,
    bq_hbm,
    bo_hbm,
    q_hbm,
    k_hbm,
    v_hbm,
    do_hbm,
    gq_out,
    gk_out,
    gv_out,
    gqkv_out,
    gout_out,
    lengths_ref,
    owner_ref,
    q_ref,
    do_ref,
    xbuf,
    bbuf,
    kbuf,
    vbuf,
    bias,
    dkv,
    dkv_in,
    act,
    act_in,
    slots,
    gq_in,
    acc,
    tbuf,
    r1,
    s1,
    r2,
    fin,
    fin_in,
    lsem,
    kv_s,
    kv_r,
    x_s,
    x_r,
    b_s,
    b_r,
    dkv_s,
    dkv_r,
    gq_s,
    gq_r,
    act_s,
    act_r,
    t_s,
    t_r,
    z_s,
    z_r,
    f_s,
    f_r,
):
    dp = lax.axis_index("dp")
    me = lax.axis_index("ctx")
    core = lax.rem(dp, 2)
    z = dp // 2
    nz = dp_size // 2
    sib = dp + 1 - 2 * core
    peers = (me, me + 1 - 2 * lax.rem(me, 2), lax.rem(me + 2, 4), 3 - me)
    zpeers = [lax.rem(z + k, nz) for k in range(nz)]
    tokens = q_ref.shape[0]
    window = 4 * tokens
    depth = bq_hbm.shape[0]
    step = depth // CHUNKS
    blk = tokens // BPD
    f32, bf16 = jnp.float32, jnp.bfloat16

    def remote(src, dst, send, recv, dev):
        return pltpu.make_async_remote_copy(
            src_ref=src, dst_ref=dst, send_sem=send, recv_sem=recv, device_id=dev, device_id_type=MESH
        )

    own_x0 = pltpu.make_async_copy(x_hbm, xbuf.at[0], lsem.at[0])
    own_x1 = pltpu.make_async_copy(g_hbm, xbuf.at[0], lsem.at[0])
    own_b0 = pltpu.make_async_copy(bq_hbm, bbuf.at[0], lsem.at[1])
    own_b1 = pltpu.make_async_copy(bo_hbm, bbuf.at[0], lsem.at[1])

    @pl.when(core == 0)
    def _():
        own_b0.start()
        own_x0.start()

    @pl.when(core == 1)
    def _():
        own_b1.start()
        own_x1.start()

    small = [
        pltpu.make_async_copy(src, dst, lsem.at[2 + n])
        for n, (src, dst) in enumerate(
            (
                (lengths_hbm, lengths_ref),
                (owner_hbm, owner_ref),
                (q_hbm, q_ref),
                (do_hbm, do_ref),
                (k_hbm, kbuf.at[me]),
                (v_hbm, vbuf.at[me]),
            )
        )
    ]
    for c in small:
        c.start()
    barrier = pltpu.get_barrier_semaphore()
    for r in (1, 2, 3):
        pl.semaphore_signal(barrier, inc=1, device_id=(dp, peers[r]), device_id_type=MESH)
    pl.semaphore_signal(barrier, inc=1, device_id=(sib, me), device_id_type=MESH)
    zp = 2 * (z + 1 - 2 * lax.rem(z, 2)) + core
    for k in range(1, nz):
        pl.semaphore_signal(
            barrier, inc=1, device_id=(2 * zpeers[k] + core, me), device_id_type=MESH
        )
    pl.semaphore_wait(barrier, 3 + 1 + nz - 1)

    kv_copies = []
    for r in (1, 2, 3):
        for i, (src, dst) in enumerate(((k_hbm, kbuf), (v_hbm, vbuf))):
            n = 2 * (r - 1) + i
            kv_copies.append(
                remote(src, dst.at[me], kv_s.at[n], kv_r.at[n], (dp, peers[r]))
            )
    for c in kv_copies:
        c.start()

    own_b0.wait()

    par = lax.rem(z, 2)

    def spot(k):
        return k + par * (CHUNKS - 1 - 2 * k)

    def rows(k):
        return pl.ds(pl.multiple_of(spot(k) * step, step), step)

    unit = CHUNKS // 4
    count = [0]

    def basis_copy(slot, k, to, dev):
        n = count[0]
        count[0] += 1
        m = (to - 1) * CHUNKS + spot(k)
        return remote(
            bbuf.at[slot, rows(k)], bbuf.at[to, rows(k)], b_s.at[n], b_r.at[m], dev
        )

    def arrived(slot, k):
        m = (slot - 1) * CHUNKS + spot(k)
        remote(
            bbuf.at[0, rows(k)], bbuf.at[slot, rows(k)], b_s.at[0], b_r.at[m], x_dev
        ).wait_recv()

    x_dev, y_dev, z_dev = (dp, peers[1]), (dp, peers[2]), (zp, me)
    groups = [list(range(g * unit, (g + 1) * unit)) for g in range(4)]
    early, late = [], []
    for k, j in zip(groups[0], groups[1]):
        early.append(basis_copy(0, k, 1, x_dev))
        early.append(basis_copy(0, j, 2, y_dev))
    for k, j in zip(groups[1] + groups[2], groups[0] + groups[3]):
        late.append(basis_copy(0, k, 1, x_dev))
        late.append(basis_copy(0, j, 2, y_dev))
    fwd_y = [basis_copy(1, k, 3, y_dev) for k in groups[0]]
    fwd_x = [basis_copy(2, k, 3, x_dev) for k in groups[1]]
    over_z1 = [basis_copy(1, k, 1, z_dev) for k in groups[0]]
    over_z2 = [basis_copy(2, k, 2, z_dev) for k in groups[1]]
    over_z3 = [basis_copy(3, k, 3, z_dev) for k in groups[0] + groups[1]]
    for c in early:
        c.start()

    sib_x0 = remote(g_hbm, xbuf.at[1], x_s, x_r, (sib, me))
    sib_x1 = remote(x_hbm, xbuf.at[1], x_s, x_r, (sib, me))

    @pl.when(core == 0)
    def _():
        sib_x0.start()

    @pl.when(core == 1)
    def _():
        sib_x1.start()

    for c in small:
        c.wait()
    pos = me * tokens + lax.broadcasted_iota(jnp.int32, (tokens, 1), 0)
    begin = jnp.zeros((tokens, 1), jnp.int32)
    end = jnp.int32(0)
    for n in range(lengths_ref.shape[1]):
        end = end + lengths_ref[0, n]
        begin = jnp.where(pos >= end, end, begin)
    key_pos = lax.broadcasted_iota(jnp.int32, (tokens, window), 1)
    bias[...] = jnp.where((key_pos <= pos) & (key_pos >= begin), 0.0, NEG_LARGE).astype(f32)
    dkv[...] = jnp.zeros_like(dkv)
    act[...] = jnp.zeros_like(act)

    for c in kv_copies:
        c.wait()

    scale = HD ** (-0.5)
    across = (((1,), (1,)), ((), ()))
    down = (((0,), (0,)), ((), ()))

    def head(h, carry):
        cols = pl.ds(pl.multiple_of(h * HD, HD), HD)
        key = kbuf[...].reshape(window, HD)
        val = vbuf[...].reshape(window, HD)
        q = q_ref[:, cols]
        do = do_ref[:, cols]
        s = lax.dot_general(q, key, across, preferred_element_type=f32) * scale + bias[...]
        top = jnp.max(s, axis=1, keepdims=True)
        e = jnp.exp(s - top)
        p = e * (1.0 / jnp.sum(e, axis=1, keepdims=True))
        w = p.astype(bf16)
        o = jnp.dot(w, val, preferred_element_type=f32).astype(bf16)
        delta = jnp.sum(do.astype(f32) * o.astype(f32), axis=1, keepdims=True)
        dprob = lax.dot_general(do, val, across, preferred_element_type=f32)
        ds = (p * (dprob - delta) * scale).astype(bf16)
        act[0, :, cols] = jnp.dot(ds, key, preferred_element_type=f32).astype(bf16)
        act[1, :, cols] = o
        dk = lax.dot_general(ds, q, down, preferred_element_type=f32)
        dv = lax.dot_general(w, do, down, preferred_element_type=f32)
        dkv[0] += dk.reshape(4, tokens, HD)
        dkv[1] += dv.reshape(4, tokens, HD)
        return carry

    lax.fori_loop(0, HQ, head, 0)

    for i in range(unit):
        arrived(1, groups[0][i])
        fwd_y[i].start()
        over_z1[i].start()
        arrived(2, groups[1][i])
        fwd_x[i].start()
        over_z2[i].start()

    dkv_copies = [
        remote(dkv.at[:, peers[r]], dkv_in.at[r - 1], dkv_s.at[r - 1], dkv_r.at[r - 1], (dp, peers[r]))
        for r in (1, 2, 3)
    ]
    for c in dkv_copies:
        c.start()

    wide = HQ * HD
    for d in range(4):
        chosen = jnp.zeros((blk, wide), f32)
        for j in range(BPD):
            piece = act[0, j * blk : (j + 1) * blk, :wide].astype(f32)
            chosen = jnp.where(owner_ref[0, me * BPD + j] == d, piece, chosen)
        slots[d] = chosen.astype(bf16)
    gq_copies = [
        remote(slots.at[peers[r]], gq_in.at[me], gq_s.at[r - 1], gq_r.at[r - 1], (dp, peers[r]))
        for r in (1, 2, 3)
    ]
    for c in gq_copies:
        c.start()
    gq_in[me] = slots[me]

    for c in dkv_copies:
        c.wait()
    for i, out in enumerate((gk_out, gv_out)):
        total = dkv[i, me] + dkv_in[0, i] + dkv_in[1, i] + dkv_in[2, i]
        total = total.astype(bf16)
        out[...] = total
        act[0, :, wide + i * HD : wide + (i + 1) * HD] = total
    act_copy = remote(act.at[1 - core], act_in, act_s, act_r, (sib, me))
    act_copy.start()

    own_x0.wait()
    sib_x0.wait()

    def add(slot, k, first=False):
        at = pl.multiple_of(peers[slot] * depth + spot(k) * step, step)
        x = xbuf[:, :, pl.ds(at, step)].reshape(2 * tokens, step)
        part = jnp.dot(x, bbuf[slot, rows(k), :], preferred_element_type=f32)
        if first:
            acc[...] = part
        else:
            acc[...] += part

    for i in range(unit):
        arrived(3, groups[0][i])
        over_z3[i].start()
        arrived(3, groups[1][i])
        over_z3[unit + i].start()
    for c in late:
        c.start()
    for k in range(CHUNKS):
        add(0, k, k == 0)
    for k in groups[0] + groups[1]:
        add(3, k)
    for k, j in zip(groups[0], groups[1]):
        add(1, k)
        add(2, j)
    for k, j in zip(groups[1], groups[0]):
        arrived(1, k)
        add(1, k)
        arrived(2, j)
        add(2, j)
    act_copy.wait()
    for c in gq_copies:
        c.wait()
    for d in range(4):
        gq_out[d * blk : (d + 1) * blk, :] = gq_in[d]
    for k, j in zip(groups[2], groups[3]):
        arrived(1, k)
        add(1, k)
        arrived(2, j)
        add(2, j)
    for k, j in zip(groups[3], groups[2]):
        arrived(1, k)
        add(1, k)
        arrived(2, j)
        add(2, j)
    for k in groups[3][::-1] + groups[2][::-1]:
        arrived(3, k)
        add(3, k)

    own_rows = acc.shape[1] // (dp_size * 4)
    per_dp = 4 * own_rows
    part = dp_size // 2
    t_copies = []
    for h in range(2):
        span = pl.ds(h * part, part)
        t_copies.append(
            [
                remote(
                    tbuf.at[span, peers[r]],
                    r1.at[r - 1, span],
                    t_s.at[3 * h + r - 1],
                    t_r.at[3 * h + r - 1],
                    (dp, peers[r]),
                )
                for r in (3, 1, 2)
            ]
        )
    for h in range(2):
        for d in range(h * part, (h + 1) * part, 2):
            left = acc[:, d * per_dp : (d + 2) * per_dp].astype(bf16)
            both = lax.dot_general(
                left[:tokens], act[core], down, preferred_element_type=f32
            ) + lax.dot_general(left[tokens:], act_in[...], down, preferred_element_type=f32)
            tbuf[d : d + 2] = both.astype(bf16).reshape(2, 4, own_rows, both.shape[1])
        for c in t_copies[h]:
            c.start()
    for c in early + late + fwd_x + fwd_y + over_z1 + over_z2 + over_z3:
        c.wait_send()
    z_copies = [
        remote(
            s1.at[zpeers[k]], r2.at[k - 1], z_s.at[k - 1], z_r.at[k - 1], (2 * zpeers[k] + core, me)
        )
        for k in range(1, nz)
    ]
    for h in range(2):
        for c in t_copies[h]:
            c.wait()
        for d in range(h * part, (h + 1) * part):
            total = tbuf[d, me].astype(f32) + r1[0, d].astype(f32)
            total = total + (r1[1, d].astype(f32) + r1[2, d].astype(f32))
            s1[d // 2, d % 2] = total.astype(bf16)
        for k in range(1, nz):

            @pl.when(zpeers[k] // (nz // 2) == h)
            def _():
                z_copies[k - 1].start()

    for c in z_copies:
        c.wait()
    total = s1[z].astype(f32)
    for k in range(1, nz):
        total = total + r2[k - 1].astype(f32)
    fin[...] = total * scale_out
    f_copy = remote(fin.at[1 - core], fin_in, f_s, f_r, (sib, me))
    f_copy.start()
    f_copy.wait()
    mine = fin[core]
    other = fin_in[...]
    gqkv_out[...] = jnp.where(core == 0, mine, other)
    gout_out[...] = jnp.where(core == 0, other, mine)[:, :wide]


def fused_shards(
    inputs,
    out_grad,
    queries,
    keys,
    values,
    attn_grad,
    doc_lengths,
    block_owner,
    basis_qkv,
    basis_out,
):
    dp_size = lax.axis_size("dp")
    nz = dp_size // 2
    tokens, width = inputs.shape
    depth, rank = basis_qkv.shape
    wide = queries.shape[1]
    cols = wide + 2 * HD
    own_rows = rank // (dp_size * 4)
    blk = tokens // BPD
    f32, bf16 = jnp.float32, jnp.bfloat16
    norm_factor = 1.0 / math.sqrt(tokens * 4 * dp_size)
    vmem = pl.BlockSpec(memory_space=pltpu.VMEM)
    hbm = pl.BlockSpec(memory_space=pl.ANY)
    dma = pltpu.SemaphoreType.DMA
    return pl.pallas_call(
        functools.partial(fused_kernel, dp_size, norm_factor),
        out_shape=(
            jax.ShapeDtypeStruct((tokens, wide), bf16),
            jax.ShapeDtypeStruct((tokens, HD), bf16),
            jax.ShapeDtypeStruct((tokens, HD), bf16),
            jax.ShapeDtypeStruct((own_rows, cols), f32),
            jax.ShapeDtypeStruct((own_rows, wide), f32),
        ),
        in_specs=[hbm] * 10,
        out_specs=[vmem] * 5,
        scratch_shapes=[
            pltpu.SMEM(doc_lengths.shape, jnp.int32),
            pltpu.SMEM(block_owner.shape, jnp.int32),
            pltpu.VMEM((tokens, wide), bf16),
            pltpu.VMEM((tokens, wide), bf16),
            pltpu.VMEM((2, tokens, width), bf16),
            pltpu.VMEM((4, depth, rank), bf16),
            pltpu.VMEM((4, tokens, HD), bf16),
            pltpu.VMEM((4, tokens, HD), bf16),
            pltpu.VMEM((tokens, 4 * tokens), f32),
            pltpu.VMEM((2, 4, tokens, HD), f32),
            pltpu.VMEM((3, 2, tokens, HD), f32),
            pltpu.VMEM((2, tokens, cols), bf16),
            pltpu.VMEM((tokens, cols), bf16),
            pltpu.VMEM((4, blk, wide), bf16),
            pltpu.VMEM((4, blk, wide), bf16),
            pltpu.VMEM((2 * tokens, rank), f32),
            pltpu.VMEM((dp_size, 4, own_rows, cols), bf16),
            pltpu.VMEM((3, dp_size, own_rows, cols), bf16),
            pltpu.VMEM((nz, 2, own_rows, cols), bf16),
            pltpu.VMEM((nz - 1, 2, own_rows, cols), bf16),
            pltpu.VMEM((2, own_rows, cols), f32),
            pltpu.VMEM((own_rows, cols), f32),
            dma((8,)),
            dma((6,)),
            dma((6,)),
            dma,
            dma,
            dma((3 * CHUNKS,)),
            dma((3 * CHUNKS,)),
            dma((3,)),
            dma((3,)),
            dma((3,)),
            dma((3,)),
            dma,
            dma,
            dma((6,)),
            dma((6,)),
            dma((nz - 1,)),
            dma((nz - 1,)),
            dma,
            dma,
        ],
        compiler_params=pltpu.CompilerParams(
            collective_id=0, has_side_effects=True, vmem_limit_bytes=60 * 1024 * 1024
        ),
        name="fused",
    )(
        doc_lengths,
        block_owner,
        inputs,
        out_grad,
        basis_qkv,
        basis_out,
        queries,
        keys,
        values,
        attn_grad,
    )


def solution(mesh):
    in_specs = (
        P(("dp", "ctx"), None),
        P(("dp", "ctx"), None),
        P(("dp", "ctx"), None),
        P(("dp", "ctx"), None),
        P(("dp", "ctx"), None),
        P(("dp", "ctx"), None),
        P("dp", None),
        P("dp", None),
        P("ctx", None),
        P("ctx", None),
    )
    out_specs = (
        P(("dp", "ctx"), None),
        P(("dp", "ctx"), None),
        P(("dp", "ctx"), None),
        P(("dp", "ctx"), None),
        P(("dp", "ctx"), None),
    )
    body = fused_shards if mesh.shape["ctx"] == 4 and mesh.shape["dp"] == 8 else shards
    return jax.shard_map(body, mesh=mesh, in_specs=in_specs, out_specs=out_specs, check_vma=False)
```

```python
import functools
import math

import jax
import jax.numpy as jnp
from jax import lax
from jax.experimental import pallas as pl
from jax.experimental.pallas import tpu as pltpu
from jax.sharding import PartitionSpec as P

HD = 128
HQ = 8
GROUPS = 1
BPD = 4


NEG_LARGE = -1e30


def doc_index_of(ends_row, positions):
    return jnp.sum((positions[:, None] >= ends_row[None, :]).astype(jnp.int32), axis=1)


def doc_start_of(ends_row, position):
    return jnp.max(jnp.where(ends_row <= position, ends_row, 0))


def slot_buffer(blocks, destination, peer_count):
    chooser = (destination[None, :] == jnp.arange(peer_count, dtype=jnp.int32)[:, None]).astype(
        blocks.dtype
    )
    return jnp.einsum("dj,jbf->dbf", chooser, blocks)


def compact_slots(received, sources, peer_count):
    chooser = (sources[:, None] == jnp.arange(peer_count, dtype=jnp.int32)[None, :]).astype(
        received.dtype
    )
    return jnp.einsum("kd,dbf->kbf", chooser, received)


def attend_group(
    query_rows,
    dout_rows,
    row_pos,
    row_docs,
    low_key,
    high_key,
    key_group,
    value_group,
    key_docs,
    key_block,
    grad_key,
    grad_value,
):
    scale_factor = HD ** (-0.5)
    block_count = key_group.shape[0] // key_block
    row_count = query_rows.shape[0]
    across = (((1,), (1,)), ((), ()))
    downward = (((0,), (0,)), ((), ()))

    def block_scores(block_id):
        begin_key = block_id * key_block
        key_piece = lax.dynamic_slice_in_dim(key_group, begin_key, key_block, 0)
        value_piece = lax.dynamic_slice_in_dim(value_group, begin_key, key_block, 0)
        piece_docs = lax.dynamic_slice_in_dim(key_docs, begin_key, key_block, 0)
        key_pos = begin_key + jnp.arange(key_block, dtype=jnp.int32)
        allowed = (row_docs[:, None] == piece_docs[None, :]) & (
            key_pos[None, :] <= row_pos[:, None]
        )
        scores = (
            lax.dot_general(query_rows, key_piece, across, preferred_element_type=jnp.float32)
            * scale_factor
        )
        return (scores, allowed, key_piece, value_piece)

    def needed(block_id):
        return (block_id * key_block <= high_key) & ((block_id + 1) * key_block > low_key)

    def stats_step(block_id, running):

        def stats_compute(stats_in):
            peak_old, total_old = stats_in
            scores, allowed, key_piece, value_piece = block_scores(block_id)
            peak_new = jnp.maximum(peak_old, jnp.max(jnp.where(allowed, scores, NEG_LARGE), axis=1))
            shifted = jnp.where(allowed, jnp.exp(scores - peak_new[:, None]), 0.0)
            return (peak_new, total_old * jnp.exp(peak_old - peak_new) + jnp.sum(shifted, axis=1))

        return lax.cond(needed(block_id), stats_compute, lambda unchanged: unchanged, running)

    start_stats = (
        jnp.full((row_count,), NEG_LARGE, jnp.float32),
        jnp.zeros((row_count,), jnp.float32),
    )
    peak_score, denom_total = lax.fori_loop(0, block_count, stats_step, start_stats)
    log_total = peak_score + jnp.log(denom_total)

    def out_step(block_id, running):

        def out_compute(acc_in):
            scores, allowed, key_piece, value_piece = block_scores(block_id)
            weights = jnp.where(allowed, jnp.exp(scores - log_total[:, None]), 0.0).astype(
                jnp.bfloat16
            )
            return acc_in + jnp.dot(weights, value_piece, preferred_element_type=jnp.float32)

        return lax.cond(needed(block_id), out_compute, lambda unchanged: unchanged, running)

    out_sums = lax.fori_loop(0, block_count, out_step, jnp.zeros((row_count, HD), jnp.float32))
    out_rows = out_sums.astype(jnp.bfloat16)
    row_delta = jnp.sum(dout_rows.astype(jnp.float32) * out_rows.astype(jnp.float32), axis=1)

    def grad_step(block_id, running):

        def grad_compute(carried):
            grad_query, key_acc, value_acc = carried
            scores, allowed, key_piece, value_piece = block_scores(block_id)
            probability = jnp.where(allowed, jnp.exp(scores - log_total[:, None]), 0.0)
            weights = probability.astype(jnp.bfloat16)
            grad_prob = lax.dot_general(
                dout_rows, value_piece, across, preferred_element_type=jnp.float32
            )
            grad_scores = (probability * (grad_prob - row_delta[:, None]) * scale_factor).astype(
                jnp.bfloat16
            )
            grad_query = grad_query + jnp.dot(
                grad_scores, key_piece, preferred_element_type=jnp.float32
            )
            begin_key = block_id * key_block
            key_update = lax.dot_general(
                grad_scores, query_rows, downward, preferred_element_type=jnp.float32
            )
            value_update = lax.dot_general(
                weights, dout_rows, downward, preferred_element_type=jnp.float32
            )
            key_acc = lax.dynamic_update_slice_in_dim(
                key_acc,
                lax.dynamic_slice_in_dim(key_acc, begin_key, key_block, 0) + key_update,
                begin_key,
                0,
            )
            value_acc = lax.dynamic_update_slice_in_dim(
                value_acc,
                lax.dynamic_slice_in_dim(value_acc, begin_key, key_block, 0) + value_update,
                begin_key,
                0,
            )
            return (grad_query, key_acc, value_acc)

        return lax.cond(needed(block_id), grad_compute, lambda unchanged: unchanged, running)

    start_grads = (jnp.zeros((row_count, HD), jnp.float32), grad_key, grad_value)
    grad_query, grad_key, grad_value = lax.fori_loop(0, block_count, grad_step, start_grads)
    return (grad_query.astype(jnp.bfloat16), out_rows, grad_key, grad_value)


def attention_backward(
    query_local, dout_local, block_starts, key_all, value_all, ends_row, block_len, key_block
):
    token_count = query_local.shape[0]
    window_len = key_all.shape[0]
    key_docs = doc_index_of(ends_row, jnp.arange(window_len, dtype=jnp.int32))
    query_view = query_local.reshape(token_count, GROUPS, HQ * HD)
    dout_view = dout_local.reshape(token_count, GROUPS, HQ * HD)
    query_groups, out_groups, key_groups, value_groups = ([], [], [], [])
    grad_key = jnp.zeros((window_len, HD), jnp.float32)
    grad_value = jnp.zeros((window_len, HD), jnp.float32)
    query_blocks = []
    out_blocks = []
    for block_id in range(BPD):
        first_pos = block_starts[block_id]
        lower_row = block_id * block_len
        query_rows = query_view[lower_row : lower_row + block_len, 0].reshape(block_len * HQ, HD)
        dout_rows = dout_view[lower_row : lower_row + block_len, 0].reshape(block_len * HQ, HD)
        row_pos = jnp.repeat(first_pos + jnp.arange(block_len, dtype=jnp.int32), HQ)
        row_docs = doc_index_of(ends_row, row_pos)
        low_key = doc_start_of(ends_row, first_pos)
        high_key = first_pos + block_len - 1
        grad_rows, out_rows, grad_key, grad_value = attend_group(
            query_rows,
            dout_rows,
            row_pos,
            row_docs,
            low_key,
            high_key,
            key_all,
            value_all,
            key_docs,
            key_block,
            grad_key,
            grad_value,
        )
        query_blocks.append(grad_rows.reshape(block_len, HQ * HD))
        out_blocks.append(out_rows.reshape(block_len, HQ * HD))
    query_groups.append(jnp.concatenate(query_blocks, axis=0))
    out_groups.append(jnp.concatenate(out_blocks, axis=0))
    key_groups.append(grad_key)
    value_groups.append(grad_value)
    return (query_groups[0], out_groups[0], key_groups[0], value_groups[0])


def shards(
    inputs,
    out_grad,
    queries,
    keys,
    values,
    attn_grad,
    doc_lengths,
    block_owner,
    basis_qkv,
    basis_out,
):
    peer_count = lax.axis_size("ctx")
    self_index = lax.axis_index("ctx")
    token_count = inputs.shape[0]
    window_len = token_count * peer_count
    block_len = token_count // BPD
    key_block = min(512, window_len)
    ends_row = jnp.cumsum(doc_lengths[0])
    owners = block_owner[0]
    input_sums = jnp.dot(
        inputs,
        lax.all_gather(basis_qkv, "ctx", axis=0, tiled=True),
        preferred_element_type=jnp.float32,
    )
    grad_sums = jnp.dot(
        out_grad,
        lax.all_gather(basis_out, "ctx", axis=0, tiled=True),
        preferred_element_type=jnp.float32,
    )
    input_proj = input_sums.astype(jnp.bfloat16)
    grad_proj = grad_sums.astype(jnp.bfloat16)
    key_all, value_all = (
        lax.all_gather(keys, "ctx", axis=0, tiled=True),
        lax.all_gather(values, "ctx", axis=0, tiled=True),
    )
    owned_mask = (owners == self_index).astype(jnp.int32)
    owned_rank = jnp.cumsum(owned_mask) - 1
    picker = (owned_mask[None, :] == 1) & (
        owned_rank[None, :] == jnp.arange(BPD, dtype=jnp.int32)[:, None]
    )
    block_numbers = jnp.arange(owners.shape[0], dtype=jnp.int32)
    owned_blocks = jnp.sum(jnp.where(picker, block_numbers[None, :], 0), axis=1)
    sources = owned_blocks // BPD
    destination = lax.dynamic_slice_in_dim(owners, self_index * BPD, BPD, 0)
    block_starts = self_index * token_count + jnp.arange(BPD, dtype=jnp.int32) * block_len
    grad_query, attn_out, key_part, value_part = attention_backward(
        queries, attn_grad, block_starts, key_all, value_all, ends_row, block_len, key_block
    )
    outgoing = slot_buffer(
        grad_query.reshape(BPD, block_len, grad_query.shape[1]), destination, peer_count
    )
    incoming = lax.all_to_all(outgoing, "ctx", split_axis=0, concat_axis=0, tiled=True)
    grad_queries = compact_slots(incoming, sources, peer_count).reshape(
        token_count, grad_query.shape[1]
    )
    query_term = jnp.einsum("tr,tc->rc", input_proj, grad_query, preferred_element_type=jnp.float32)
    out_term = jnp.einsum("tr,tc->rc", grad_proj, attn_out, preferred_element_type=jnp.float32)
    key_sums, value_sums = (
        lax.psum_scatter(key_part, "ctx", scatter_dimension=0, tiled=True),
        lax.psum_scatter(value_part, "ctx", scatter_dimension=0, tiled=True),
    )
    grad_keys = key_sums.astype(jnp.bfloat16)
    grad_values = value_sums.astype(jnp.bfloat16)
    norm_factor = 1.0 / math.sqrt(token_count * peer_count * lax.axis_size("dp"))
    qkv_term = (
        jnp.concatenate(
            [
                query_term,
                jnp.einsum("tr,tc->rc", input_proj, grad_keys, preferred_element_type=jnp.float32),
                jnp.einsum(
                    "tr,tc->rc", input_proj, grad_values, preferred_element_type=jnp.float32
                ),
            ],
            axis=1,
        )
        * norm_factor
    )
    galore_qkv, galore_out = (
        lax.psum_scatter(qkv_term, ("dp", "ctx"), scatter_dimension=0, tiled=True),
        lax.psum_scatter(out_term * norm_factor, ("dp", "ctx"), scatter_dimension=0, tiled=True),
    )
    return (grad_queries, grad_keys, grad_values, galore_qkv, galore_out)


MESH = pl.DeviceIdType.MESH
CHUNKS = 8


def fused_kernel(
    dp_size,
    scale_out,
    lengths_hbm,
    owner_hbm,
    x_hbm,
    g_hbm,
    bq_hbm,
    bo_hbm,
    q_hbm,
    k_hbm,
    v_hbm,
    do_hbm,
    gq_out,
    gk_out,
    gv_out,
    gqkv_out,
    gout_out,
    lengths_ref,
    owner_ref,
    q_ref,
    do_ref,
    xbuf,
    bbuf,
    kbuf,
    vbuf,
    bias,
    dkv,
    dkv_in,
    act,
    act_in,
    slots,
    gq_in,
    acc,
    tbuf,
    r1,
    s1,
    r2,
    fin,
    fin_in,
    lsem,
    kv_s,
    kv_r,
    x_s,
    x_r,
    b_s,
    b_r,
    dkv_s,
    dkv_r,
    gq_s,
    gq_r,
    act_s,
    act_r,
    t_s,
    t_r,
    z_s,
    z_r,
    f_s,
    f_r,
):
    dp = lax.axis_index("dp")
    me = lax.axis_index("ctx")
    core = lax.rem(dp, 2)
    z = dp // 2
    nz = dp_size // 2
    sib = dp + 1 - 2 * core
    peers = (me, me + 1 - 2 * lax.rem(me, 2), lax.rem(me + 2, 4), 3 - me)
    zpeers = [lax.rem(z + k, nz) for k in range(nz)]
    tokens = q_ref.shape[0]
    window = 4 * tokens
    depth = bq_hbm.shape[0]
    step = depth // CHUNKS
    blk = tokens // BPD
    f32, bf16 = jnp.float32, jnp.bfloat16

    def remote(src, dst, send, recv, dev):
        return pltpu.make_async_remote_copy(
            src_ref=src, dst_ref=dst, send_sem=send, recv_sem=recv, device_id=dev, device_id_type=MESH
        )

    own_x0 = pltpu.make_async_copy(x_hbm, xbuf.at[0], lsem.at[0])
    own_x1 = pltpu.make_async_copy(g_hbm, xbuf.at[0], lsem.at[0])
    own_b0 = pltpu.make_async_copy(bq_hbm, bbuf.at[0], lsem.at[1])
    own_b1 = pltpu.make_async_copy(bo_hbm, bbuf.at[0], lsem.at[1])

    @pl.when(core == 0)
    def _():
        own_b0.start()
        own_x0.start()

    @pl.when(core == 1)
    def _():
        own_b1.start()
        own_x1.start()

    small = [
        pltpu.make_async_copy(src, dst, lsem.at[2 + n])
        for n, (src, dst) in enumerate(
            (
                (lengths_hbm, lengths_ref),
                (owner_hbm, owner_ref),
                (q_hbm, q_ref),
                (do_hbm, do_ref),
                (k_hbm, kbuf.at[me]),
                (v_hbm, vbuf.at[me]),
            )
        )
    ]
    for c in small:
        c.start()
    barrier = pltpu.get_barrier_semaphore()
    for r in (1, 2, 3):
        pl.semaphore_signal(barrier, inc=1, device_id=(dp, peers[r]), device_id_type=MESH)
    pl.semaphore_signal(barrier, inc=1, device_id=(sib, me), device_id_type=MESH)
    zp = 2 * (z + 1 - 2 * lax.rem(z, 2)) + core
    for k in range(1, nz):
        pl.semaphore_signal(
            barrier, inc=1, device_id=(2 * zpeers[k] + core, me), device_id_type=MESH
        )
    pl.semaphore_wait(barrier, 3 + 1 + nz - 1)

    kv_copies = []
    for r in (1, 2, 3):
        for i, (src, dst) in enumerate(((k_hbm, kbuf), (v_hbm, vbuf))):
            n = 2 * (r - 1) + i
            kv_copies.append(
                remote(src, dst.at[me], kv_s.at[n], kv_r.at[n], (dp, peers[r]))
            )
    for c in kv_copies:
        c.start()

    own_b0.wait()

    par = lax.rem(z, 2)

    def spot(k):
        return k + par * (CHUNKS - 1 - 2 * k)

    def rows(k):
        return pl.ds(pl.multiple_of(spot(k) * step, step), step)

    unit = CHUNKS // 4
    count = [0]

    def basis_copy(slot, k, to, dev):
        n = count[0]
        count[0] += 1
        m = (to - 1) * CHUNKS + spot(k)
        return remote(
            bbuf.at[slot, rows(k)], bbuf.at[to, rows(k)], b_s.at[n], b_r.at[m], dev
        )

    def arrived(slot, k):
        m = (slot - 1) * CHUNKS + spot(k)
        remote(
            bbuf.at[0, rows(k)], bbuf.at[slot, rows(k)], b_s.at[0], b_r.at[m], x_dev
        ).wait_recv()

    x_dev, y_dev, z_dev = (dp, peers[1]), (dp, peers[2]), (zp, me)
    groups = [list(range(g * unit, (g + 1) * unit)) for g in range(4)]
    early, late = [], []
    for k, j in zip(groups[0], groups[1]):
        early.append(basis_copy(0, k, 1, x_dev))
        early.append(basis_copy(0, j, 2, y_dev))
    for k, j in zip(groups[1] + groups[2], groups[0] + groups[3]):
        late.append(basis_copy(0, k, 1, x_dev))
        late.append(basis_copy(0, j, 2, y_dev))
    fwd_y = [basis_copy(1, k, 3, y_dev) for k in groups[0]]
    fwd_x = [basis_copy(2, k, 3, x_dev) for k in groups[1]]
    over_z1 = [basis_copy(1, k, 1, z_dev) for k in groups[0]]
    over_z2 = [basis_copy(2, k, 2, z_dev) for k in groups[1]]
    over_z3 = [basis_copy(3, k, 3, z_dev) for k in groups[0] + groups[1]]
    for c in early:
        c.start()

    sib_x0 = remote(g_hbm, xbuf.at[1], x_s, x_r, (sib, me))
    sib_x1 = remote(x_hbm, xbuf.at[1], x_s, x_r, (sib, me))

    @pl.when(core == 0)
    def _():
        sib_x0.start()

    @pl.when(core == 1)
    def _():
        sib_x1.start()

    for c in small:
        c.wait()
    pos = me * tokens + lax.broadcasted_iota(jnp.int32, (tokens, 1), 0)
    begin = jnp.zeros((tokens, 1), jnp.int32)
    end = jnp.int32(0)
    for n in range(lengths_ref.shape[1]):
        end = end + lengths_ref[0, n]
        begin = jnp.where(pos >= end, end, begin)
    key_pos = lax.broadcasted_iota(jnp.int32, (tokens, window), 1)
    bias[...] = jnp.where((key_pos <= pos) & (key_pos >= begin), 0.0, NEG_LARGE).astype(f32)
    dkv[...] = jnp.zeros_like(dkv)
    act[...] = jnp.zeros_like(act)

    for c in kv_copies:
        c.wait()

    scale = HD ** (-0.5)
    across = (((1,), (1,)), ((), ()))
    down = (((0,), (0,)), ((), ()))

    def head(h, carry):
        cols = pl.ds(pl.multiple_of(h * HD, HD), HD)
        key = kbuf[...].reshape(window, HD)
        val = vbuf[...].reshape(window, HD)
        q = q_ref[:, cols]
        do = do_ref[:, cols]
        s = lax.dot_general(q, key, across, preferred_element_type=f32) * scale + bias[...]
        top = jnp.max(s, axis=1, keepdims=True)
        e = jnp.exp(s - top)
        p = e * (1.0 / jnp.sum(e, axis=1, keepdims=True))
        w = p.astype(bf16)
        o = jnp.dot(w, val, preferred_element_type=f32).astype(bf16)
        delta = jnp.sum(do.astype(f32) * o.astype(f32), axis=1, keepdims=True)
        dprob = lax.dot_general(do, val, across, preferred_element_type=f32)
        ds = (p * (dprob - delta) * scale).astype(bf16)
        act[0, :, cols] = jnp.dot(ds, key, preferred_element_type=f32).astype(bf16)
        act[1, :, cols] = o
        dk = lax.dot_general(ds, q, down, preferred_element_type=f32)
        dv = lax.dot_general(w, do, down, preferred_element_type=f32)
        dkv[0] += dk.reshape(4, tokens, HD)
        dkv[1] += dv.reshape(4, tokens, HD)
        return carry

    lax.fori_loop(0, HQ, head, 0)

    for i in range(unit):
        arrived(1, groups[0][i])
        fwd_y[i].start()
        over_z1[i].start()
        arrived(2, groups[1][i])
        fwd_x[i].start()
        over_z2[i].start()

    dkv_copies = [
        remote(dkv.at[:, peers[r]], dkv_in.at[r - 1], dkv_s.at[r - 1], dkv_r.at[r - 1], (dp, peers[r]))
        for r in (1, 2, 3)
    ]
    for c in dkv_copies:
        c.start()

    wide = HQ * HD
    for d in range(4):
        chosen = jnp.zeros((blk, wide), f32)
        for j in range(BPD):
            piece = act[0, j * blk : (j + 1) * blk, :wide].astype(f32)
            chosen = jnp.where(owner_ref[0, me * BPD + j] == d, piece, chosen)
        slots[d] = chosen.astype(bf16)
    gq_copies = [
        remote(slots.at[peers[r]], gq_in.at[me], gq_s.at[r - 1], gq_r.at[r - 1], (dp, peers[r]))
        for r in (1, 2, 3)
    ]
    for c in gq_copies:
        c.start()
    gq_in[me] = slots[me]

    for c in dkv_copies:
        c.wait()
    for i, out in enumerate((gk_out, gv_out)):
        total = dkv[i, me] + dkv_in[0, i] + dkv_in[1, i] + dkv_in[2, i]
        total = total.astype(bf16)
        out[...] = total
        act[0, :, wide + i * HD : wide + (i + 1) * HD] = total
    act_copy = remote(act.at[1 - core], act_in, act_s, act_r, (sib, me))
    act_copy.start()

    own_x0.wait()
    sib_x0.wait()

    def add(slot, k, first=False):
        at = pl.multiple_of(peers[slot] * depth + spot(k) * step, step)
        x = xbuf[:, :, pl.ds(at, step)].reshape(2 * tokens, step)
        part = jnp.dot(x, bbuf[slot, rows(k), :], preferred_element_type=f32)
        if first:
            acc[...] = part
        else:
            acc[...] += part

    for i in range(unit):
        arrived(3, groups[0][i])
        over_z3[i].start()
        arrived(3, groups[1][i])
        over_z3[unit + i].start()
    for c in late:
        c.start()
    for k in range(CHUNKS):
        add(0, k, k == 0)
    for k in groups[0] + groups[1]:
        add(3, k)
    for k, j in zip(groups[0], groups[1]):
        add(1, k)
        add(2, j)
    for k, j in zip(groups[1], groups[0]):
        arrived(1, k)
        add(1, k)
        arrived(2, j)
        add(2, j)
    act_copy.wait()
    for c in gq_copies:
        c.wait()
    for d in range(4):
        gq_out[d * blk : (d + 1) * blk, :] = gq_in[d]
    for k, j in zip(groups[2], groups[3]):
        arrived(1, k)
        add(1, k)
        arrived(2, j)
        add(2, j)
    for k, j in zip(groups[3], groups[2]):
        arrived(1, k)
        add(1, k)
        arrived(2, j)
        add(2, j)
    for k in groups[3][::-1] + groups[2][::-1]:
        arrived(3, k)
        add(3, k)

    own_rows = acc.shape[1] // (dp_size * 4)
    per_dp = 4 * own_rows
    part = dp_size // 4
    t_copies = []
    for h in range(4):
        span = pl.ds(h * part, part)
        t_copies.append(
            [
                remote(
                    tbuf.at[span, peers[r]],
                    r1.at[r - 1, span],
                    t_s.at[3 * h + r - 1],
                    t_r.at[3 * h + r - 1],
                    (dp, peers[r]),
                )
                for r in (3, 1, 2)
            ]
        )
    for h in range(4):
        for d in range(h * part, (h + 1) * part, 2):
            left = acc[:, d * per_dp : (d + 2) * per_dp].astype(bf16)
            both = lax.dot_general(
                left[:tokens], act[core], down, preferred_element_type=f32
            ) + lax.dot_general(left[tokens:], act_in[...], down, preferred_element_type=f32)
            tbuf[d : d + 2] = both.astype(bf16).reshape(2, 4, own_rows, both.shape[1])
        for c in t_copies[h]:
            c.start()
    for c in early + late + fwd_x + fwd_y + over_z1 + over_z2 + over_z3:
        c.wait_send()
    z_copies = [
        remote(
            s1.at[zpeers[k]], r2.at[k - 1], z_s.at[k - 1], z_r.at[k - 1], (2 * zpeers[k] + core, me)
        )
        for k in range(1, nz)
    ]
    for h in range(4):
        for c in t_copies[h]:
            c.wait()
        for d in range(h * part, (h + 1) * part):
            total = tbuf[d, me].astype(f32) + r1[0, d].astype(f32)
            total = total + (r1[1, d].astype(f32) + r1[2, d].astype(f32))
            s1[d // 2, d % 2] = total.astype(bf16)
        for k in range(1, nz):

            @pl.when(zpeers[k] // (nz // 4) == h)
            def _():
                z_copies[k - 1].start()

    for c in z_copies:
        c.wait()
    total = s1[z].astype(f32)
    for k in range(1, nz):
        total = total + r2[k - 1].astype(f32)
    fin[...] = total * scale_out
    f_copy = remote(fin.at[1 - core], fin_in, f_s, f_r, (sib, me))
    f_copy.start()
    f_copy.wait()
    mine = fin[core]
    other = fin_in[...]
    gqkv_out[...] = jnp.where(core == 0, mine, other)
    gout_out[...] = jnp.where(core == 0, other, mine)[:, :wide]


def fused_shards(
    inputs,
    out_grad,
    queries,
    keys,
    values,
    attn_grad,
    doc_lengths,
    block_owner,
    basis_qkv,
    basis_out,
):
    dp_size = lax.axis_size("dp")
    nz = dp_size // 2
    tokens, width = inputs.shape
    depth, rank = basis_qkv.shape
    wide = queries.shape[1]
    cols = wide + 2 * HD
    own_rows = rank // (dp_size * 4)
    blk = tokens // BPD
    f32, bf16 = jnp.float32, jnp.bfloat16
    norm_factor = 1.0 / math.sqrt(tokens * 4 * dp_size)
    vmem = pl.BlockSpec(memory_space=pltpu.VMEM)
    hbm = pl.BlockSpec(memory_space=pl.ANY)
    dma = pltpu.SemaphoreType.DMA
    return pl.pallas_call(
        functools.partial(fused_kernel, dp_size, norm_factor),
        out_shape=(
            jax.ShapeDtypeStruct((tokens, wide), bf16),
            jax.ShapeDtypeStruct((tokens, HD), bf16),
            jax.ShapeDtypeStruct((tokens, HD), bf16),
            jax.ShapeDtypeStruct((own_rows, cols), f32),
            jax.ShapeDtypeStruct((own_rows, wide), f32),
        ),
        in_specs=[hbm] * 10,
        out_specs=[vmem] * 5,
        scratch_shapes=[
            pltpu.SMEM(doc_lengths.shape, jnp.int32),
            pltpu.SMEM(block_owner.shape, jnp.int32),
            pltpu.VMEM((tokens, wide), bf16),
            pltpu.VMEM((tokens, wide), bf16),
            pltpu.VMEM((2, tokens, width), bf16),
            pltpu.VMEM((4, depth, rank), bf16),
            pltpu.VMEM((4, tokens, HD), bf16),
            pltpu.VMEM((4, tokens, HD), bf16),
            pltpu.VMEM((tokens, 4 * tokens), f32),
            pltpu.VMEM((2, 4, tokens, HD), f32),
            pltpu.VMEM((3, 2, tokens, HD), f32),
            pltpu.VMEM((2, tokens, cols), bf16),
            pltpu.VMEM((tokens, cols), bf16),
            pltpu.VMEM((4, blk, wide), bf16),
            pltpu.VMEM((4, blk, wide), bf16),
            pltpu.VMEM((2 * tokens, rank), f32),
            pltpu.VMEM((dp_size, 4, own_rows, cols), bf16),
            pltpu.VMEM((3, dp_size, own_rows, cols), bf16),
            pltpu.VMEM((nz, 2, own_rows, cols), bf16),
            pltpu.VMEM((nz - 1, 2, own_rows, cols), bf16),
            pltpu.VMEM((2, own_rows, cols), f32),
            pltpu.VMEM((own_rows, cols), f32),
            dma((8,)),
            dma((6,)),
            dma((6,)),
            dma,
            dma,
            dma((3 * CHUNKS,)),
            dma((3 * CHUNKS,)),
            dma((3,)),
            dma((3,)),
            dma((3,)),
            dma((3,)),
            dma,
            dma,
            dma((12,)),
            dma((12,)),
            dma((nz - 1,)),
            dma((nz - 1,)),
            dma,
            dma,
        ],
        compiler_params=pltpu.CompilerParams(
            collective_id=0, has_side_effects=True, vmem_limit_bytes=60 * 1024 * 1024
        ),
        name="fused",
    )(
        doc_lengths,
        block_owner,
        inputs,
        out_grad,
        basis_qkv,
        basis_out,
        queries,
        keys,
        values,
        attn_grad,
    )


def solution(mesh):
    in_specs = (
        P(("dp", "ctx"), None),
        P(("dp", "ctx"), None),
        P(("dp", "ctx"), None),
        P(("dp", "ctx"), None),
        P(("dp", "ctx"), None),
        P(("dp", "ctx"), None),
        P("dp", None),
        P("dp", None),
        P("ctx", None),
        P("ctx", None),
    )
    out_specs = (
        P(("dp", "ctx"), None),
        P(("dp", "ctx"), None),
        P(("dp", "ctx"), None),
        P(("dp", "ctx"), None),
        P(("dp", "ctx"), None),
    )
    body = fused_shards if mesh.shape["ctx"] == 4 and mesh.shape["dp"] == 8 else shards
    return jax.shard_map(body, mesh=mesh, in_specs=in_specs, out_specs=out_specs, check_vma=False)
```
